32 devices in a mesh: page: 32 (over z, y, x, core), head: 1.
Axes of the slice: x: 2, y: 2, z: 4, core: 2. Of those that a mesh axis runs over, the one named last changes fastest.
Arguments:
- hidden: bfloat16 [12288, 4096], P('page'), may hold values from -6 to 6
- attention_norm_gain: bfloat16 [4096], replicated, may hold values from 0.25 to 1.75
- wq: bfloat16 [4096, 4096], P('page', 'head'), may hold values from -0.09375 to 0.09375
- adapter_down_weight: bfloat16 [4096, 512], P('head', 'page'), may hold values from -0.09375 to 0.09375
- adapter_up_weight: bfloat16 [512, 4096], P('page', 'head'), may hold values from -0.75 to 0.75
- key_value_cache: bfloat16 [12288, 2, 1024], P('page', None, 'head'), may hold values from -110 to 110
- logical_page_table: int32 [32, 3], P('page'), may hold values from 0 to 2, each once within a row
- lengths: int32 [8], replicated, may hold values from 1 to 3072, 12288 in all
- prompt_adapter_index: int32 [8], replicated, may hold values from 0 to 31
Outputs:
- queries: bfloat16 [12288, 4096], P('page', 'head')
- attended: bfloat16 [12288, 4096], P('page', 'head')
The draws below stay inside these ranges and needn't reach their ends.
Inputs may be any that keep to these rules, and one draw needn't show every extreme that they name: The lengths sum to 12288 and the longest is exactly 3072. `logical_page_table`: each row is a permutation of the page slots of one index of page.
All inputs are finite; a program needn't handle non-finite values.
Results may differ from the reference program's by a relative error of at most 0.012.
The reference program's roundings to bfloat16 on the way count: a program that leaves them out, or rounds other values in their place, can miss the bound.
Values may be sent and summed in bfloat16 or wider, within the bound.
No kernel may reach another device: no remote copies, remote signals or barrier semaphores. Data moves between devices by JAX's collectives and lax.ppermute only.
A program may use at most 320 MiB of HBM per device.

```python
import math
import jax
import jax.numpy as jnp
import numpy as np
from jax import lax

MODEL_WIDTH = 4096
QUERY_HEADS = 32
KVH = 8
HEAD_WIDTH = 128
ADAPTER_RANK = 16
TOK_DEV = 384
PAGE = 128
SPAN = 8
ADAPTER_TOTAL = 32
TOKEN_TOTAL = 12288
REQUESTS = 8
PAGES_DEV = 3
N_PAGE = 32


def draw_key_value_cache(key, part):
    first_key = jax.random.fold_in(key, 0)
    output_shape = (TOKEN_TOTAL, 2, KVH * HEAD_WIDTH)
    values = jnp.clip(jax.random.normal(first_key, output_shape, jnp.float32), -4.0, 4.0)
    return values.astype(jnp.bfloat16)


def touch_ends(array, stream_key, smallest, largest):
    longest = array.shape.index(max(array.shape))
    spots = []
    for shift in (0, 1):
        where = [jax.random.randint(jax.random.fold_in(stream_key, axis), (), 0, length) for axis, length in enumerate(array.shape)]
        where[longest] = (where[longest] + shift) % array.shape[longest]
        spots.append(tuple(where))
    return array.at[spots[0]].set(smallest).at[spots[1]].set(largest)


def levels(rng, shape, cuts, smallest, top_value):
    gain = 1.0
    for position, shards_of in cuts:
        heights = jax.random.uniform(jax.random.fold_in(jax.random.fold_in(rng, 6), position), (shards_of,), jnp.float32, smallest / len(cuts), top_value / len(cuts))
        gain = gain * jnp.repeat(jnp.exp(heights), shape[position] // shards_of).reshape((-1,) + (1,) * (len(shape) - 1 - position))
    return gain


def rank_table(amount, slope):
    weights = [(1 << 20) // math.isqrt(standing ** slope) + 1 for standing in range(1, amount + 1)]
    scale = 1 + sum(weights) // (1 << 30)
    return np.cumsum(np.array([max(1, weight // scale) for weight in weights]))


def ranked_ids(rng, extent, amount, slope):
    table = rank_table(amount, slope)
    lot = jax.random.randint(jax.random.fold_in(rng, 1), extent, 0, int(table[amount - 1]))
    grade = jnp.searchsorted(jnp.asarray(table, jnp.int32), lot, side="right")
    return jax.random.permutation(jax.random.fold_in(rng, 2), amount)[grade].astype(jnp.int32)


def profile(number_of, total, bound, slope):
    loads = [(1 << 20) // math.isqrt(grade ** slope) + 1 for grade in range(2, number_of + 1)]
    rest, given = total - bound - (number_of - 1), [1] * (number_of - 1)
    while rest > 0:
        free = [i for i in range(number_of - 1) if given[i] < bound]
        pool, left = sum([loads[i] for i in free]), rest
        for i in free:
            more = min(bound - given[i], max(1, left * loads[i] // pool), rest)
            given[i] = given[i] + more
            rest = rest - more
    return np.array([bound] + given)


def ragged(key, count, total, reach, slope):
    if count == 2:
        one = jax.random.randint(key, (), max(1, total - reach), min(reach, total - 1) + 1)
        return jnp.stack([one, total - one])
    tallies = jnp.asarray(profile(count, total, reach, slope), jnp.int32)
    pairs = (count - 1) // 2
    donor, receiver = tallies[1:1 + 2 * pairs:2], tallies[2:2 + 2 * pairs:2]
    slack = jnp.minimum(donor - 1, reach - receiver)
    passed = jax.random.randint(jax.random.fold_in(key, 1), (pairs,), 0, 1 << 20) % (slack + 1)
    tallies = tallies.at[1:1 + 2 * pairs:2].set(donor - passed).at[2:2 + 2 * pairs:2].set(receiver + passed)
    return tallies[jax.random.permutation(jax.random.fold_in(key, 2), count)]


def centred(stream_key, shape, spread, most, shards=(), held_as=jnp.bfloat16):
    array = spread * jax.random.normal(stream_key, shape, jnp.float32)
    if shards:
        array = array * levels(stream_key, shape, shards, -0.22, 0.18)
    return jnp.clip(array, -most, most).astype(held_as)


def setup_inputs(seed: int = 0) -> dict:
    seeds = jax.random.split(jax.random.key(seed), 10)
    return {
        "hidden": centred(seeds[0], (TOKEN_TOTAL, MODEL_WIDTH), 1.0, 6.0, ((0, 32),)),
        "attention_norm_gain": jnp.clip(1.0 + 0.15 * jax.random.normal(seeds[1], (MODEL_WIDTH,), jnp.float32), 0.25, 1.75).astype(jnp.bfloat16),
        "wq": centred(seeds[2], (MODEL_WIDTH, QUERY_HEADS * HEAD_WIDTH), MODEL_WIDTH ** -0.5, 0.09375, ((0, 32),)),
        "adapter_down_weight": centred(seeds[3], (MODEL_WIDTH, ADAPTER_TOTAL * ADAPTER_RANK), MODEL_WIDTH ** -0.5, 0.09375, ((1, 32),)),
        "adapter_up_weight": centred(seeds[4], (ADAPTER_TOTAL * ADAPTER_RANK, QUERY_HEADS * HEAD_WIDTH), (4 * ADAPTER_RANK) ** -0.5, 0.75, ((0, 32),)),
        "key_value_cache": draw_key_value_cache(jax.random.fold_in(seeds[9], 71), 0),
        "logical_page_table": jax.vmap(lambda own: jax.random.permutation(own, PAGES_DEV))(jax.random.split(seeds[6], N_PAGE)).reshape((N_PAGE, PAGES_DEV)).astype(jnp.int32),
        "lengths": ragged(seeds[7], REQUESTS, TOKEN_TOTAL, SPAN * TOK_DEV, 2).astype(jnp.int32),
        "prompt_adapter_index": touch_ends(ranked_ids(seeds[8], (REQUESTS,), ADAPTER_TOTAL, 2), jax.random.fold_in(seeds[8], 3), 0, ADAPTER_TOTAL - 1).astype(jnp.int32),
    }


EPSILON = 1e-05
ROPE_BASE = 500000.0

def apply_rotation(values_f, token_position):
    half = HEAD_WIDTH // 2
    inverse = ROPE_BASE ** (-(jnp.arange(half, dtype=jnp.float32) * 2.0 / HEAD_WIDTH))
    angle = token_position.astype(jnp.float32)[:, None] * inverse[None, :]
    cosine = jnp.cos(angle)[:, None, :]
    sine = jnp.sin(angle)[:, None, :]
    first = values_f[..., :half]
    second = values_f[..., half:]
    return jnp.concatenate([first * cosine - second * sine, second * cosine + first * sine], axis=-1)

def reference(hidden, attention_norm_gain, wq, adapter_down_weight, adapter_up_weight, key_value_cache, logical_page_table, lengths, prompt_adapter_index):
    x = hidden.astype(jnp.float32)
    scale_rows = lax.rsqrt(lax.optimization_barrier(jnp.mean(x * x, axis=-1, keepdims=True)) + EPSILON)
    normed_input = (x * scale_rows * attention_norm_gain.astype(jnp.float32)).astype(jnp.bfloat16)
    ends = jnp.cumsum(lengths).astype(jnp.int32)
    starts = (ends - lengths).astype(jnp.int32)
    token = jnp.arange(TOKEN_TOTAL, dtype=jnp.int32)
    member = (token[:, None] >= starts[None, :]) & (token[:, None] < ends[None, :])
    tok_start = lax.optimization_barrier(jnp.sum(jnp.where(member, starts[None, :], 0), axis=1)).astype(jnp.int32)
    tok_adapter = lax.optimization_barrier(jnp.sum(jnp.where(member, prompt_adapter_index[None, :], 0), axis=1)).astype(jnp.int32)
    token_position = token - tok_start
    base_query = jnp.dot(normed_input, wq, preferred_element_type=jnp.float32)
    partial_every_token = jnp.dot(normed_input, adapter_down_weight, preferred_element_type=jnp.float32).reshape(TOKEN_TOTAL, ADAPTER_TOTAL, ADAPTER_RANK)
    pick = tok_adapter[:, None] == jnp.arange(ADAPTER_TOTAL, dtype=jnp.int32)[None, :]
    shrunk = lax.optimization_barrier(jnp.sum(jnp.where(pick[:, :, None], partial_every_token, 0.0), axis=1)).astype(jnp.bfloat16)
    spread_heads = jnp.where(pick[:, :, None], shrunk[:, None, :], jnp.zeros((), jnp.bfloat16)).reshape(TOKEN_TOTAL, ADAPTER_TOTAL * ADAPTER_RANK)
    adapter_delta = jnp.dot(spread_heads, adapter_up_weight, preferred_element_type=jnp.float32)
    queries = apply_rotation((base_query + adapter_delta).reshape(TOKEN_TOTAL, QUERY_HEADS, HEAD_WIDTH), token_position).astype(jnp.bfloat16)
    paged = key_value_cache.reshape(N_PAGE, PAGES_DEV, PAGE, 2, KVH * HEAD_WIDTH)
    ordered = jax.vmap(lambda blocks, table: jnp.take(blocks, table, axis=0))(paged, logical_page_table)
    ordered = ordered.reshape(TOKEN_TOTAL, 2, KVH, HEAD_WIDTH)
    margin = SPAN * TOK_DEV
    padded = jnp.concatenate([jnp.zeros((margin, 2, KVH, HEAD_WIDTH), ordered.dtype), ordered], axis=0)
    inv_scale = 1.0 / math.sqrt(HEAD_WIDTH)

    def one_block(index):
        first = (index * TOK_DEV).astype(jnp.int32)
        query_block = lax.dynamic_slice_in_dim(queries, first, TOK_DEV, 0).astype(jnp.float32)
        query_block = query_block.reshape(TOK_DEV, KVH, QUERY_HEADS // KVH, HEAD_WIDTH)
        window = lax.dynamic_slice_in_dim(padded, first, margin + TOK_DEV, 0).astype(jnp.float32)
        query_start = lax.dynamic_slice_in_dim(tok_start, first, TOK_DEV, 0)
        query_index = first + jnp.arange(TOK_DEV, dtype=jnp.int32)
        key_index = first - margin + jnp.arange(margin + TOK_DEV, dtype=jnp.int32)
        visible = (key_index[None, :] >= query_start[:, None]) & (key_index[None, :] <= query_index[:, None])
        scores = jnp.einsum('tkgd,skd->kgts', query_block, window[:, 0]) * inv_scale
        scores = jnp.where(visible[None, None], scores, -jnp.inf)
        top = lax.optimization_barrier(jnp.max(scores, axis=-1, keepdims=True))
        expo = jnp.exp(scores - top)
        weights = (expo / lax.optimization_barrier(jnp.sum(expo, axis=-1, keepdims=True))).astype(jnp.bfloat16)
        mixed = jnp.einsum('kgts,skd->tkgd', weights.astype(jnp.float32), window[:, 1])
        return mixed.reshape(TOK_DEV, QUERY_HEADS * HEAD_WIDTH).astype(jnp.bfloat16)
    attended = lax.map(one_block, jnp.arange(N_PAGE, dtype=jnp.int32)).reshape(TOKEN_TOTAL, QUERY_HEADS * HEAD_WIDTH)
    return (queries.reshape(TOKEN_TOTAL, QUERY_HEADS * HEAD_WIDTH), attended)
```

```python
import functools
import math

import jax
import jax.numpy as jnp
from jax import lax
from jax.experimental import pallas as pl
from jax.experimental.pallas import tpu as pltpu
from jax.sharding import PartitionSpec as P

HEAD_WIDTH = 128
ADAPTER_RANK = 16


EPSILON = 1e-05
ROPE_BASE = 500000.0
KEY_TILE = 512
TOKEN_TILE = 128
LOWEST = -1e30


def from_behind(value, axis, steps):
    count = lax.axis_size(axis)
    leading, last = (max(0, -steps), min(count, count - steps))
    return lax.ppermute(value, axis, [(source, source + steps) for source in range(leading, last)])


def apply_rotation(values_f, token_position, head_size):
    half = head_size // 2
    inverse = ROPE_BASE ** (-(jnp.arange(half, dtype=jnp.float32) * 2.0 / head_size))
    angle = token_position.astype(jnp.float32)[:, None] * inverse[None, :]
    cosine = jnp.cos(angle)[:, None, :]
    sine = jnp.sin(angle)[:, None, :]
    first = values_f[..., :half]
    second = values_f[..., half:]
    return jnp.concatenate(
        [first * cosine - second * sine, second * cosine + first * sine], axis=-1
    )


def score_block(query, keyblock):
    return lax.dot_general(
        query, keyblock, (((1,), (1,)), ((), ())), preferred_element_type=jnp.float32
    )


def mix_block(weights, valueblock):
    return jnp.dot(weights, valueblock, preferred_element_type=jnp.float32)


def normalize(scores, visible, inv_scale):
    scores = jnp.where(visible, scores * inv_scale, -jnp.inf)
    top = jnp.max(scores, axis=-1, keepdims=True)
    expo = jnp.exp(scores - top)
    return (expo / jnp.sum(expo, axis=-1, keepdims=True)).astype(jnp.bfloat16)


def body(
    hidden,
    attention_norm_gain,
    wq,
    adapter_down_weight,
    adapter_up_weight,
    key_value_cache,
    logical_page_table,
    lengths,
    prompt_adapter_index,
):
    token_device_rows = hidden.shape[0]
    page_index = lax.axis_index("page")
    head_index = lax.axis_index("head")
    span_count = lax.axis_size("page") // 4
    x = hidden.astype(jnp.float32)
    scale_rows = lax.rsqrt(jnp.mean(x * x, axis=-1, keepdims=True) + EPSILON)
    normed_input = (x * scale_rows * attention_norm_gain.astype(jnp.float32)).astype(jnp.bfloat16)
    ends = jnp.cumsum(lengths)
    starts = ends - lengths
    token = page_index * token_device_rows + jnp.arange(token_device_rows, dtype=jnp.int32)
    member = (token[:, None] >= starts[None, :]) & (token[:, None] < ends[None, :])
    tok_start = jnp.sum(jnp.where(member, starts[None, :], 0), axis=1)
    tok_adapter = jnp.sum(jnp.where(member, prompt_adapter_index[None, :], 0), axis=1)
    token_position = token - tok_start
    q_cols = wq.shape[1]
    base_query = jnp.dot(
        normed_input,
        lax.all_gather(wq, "page", axis=0, tiled=True),
        preferred_element_type=jnp.float32,
    )
    shrink_all, expand_every_token = (
        lax.all_gather(adapter_down_weight, "page", axis=1, tiled=True),
        lax.all_gather(adapter_up_weight, "page", axis=0, tiled=True),
    )
    adapter_count = shrink_all.shape[1] // ADAPTER_RANK
    feature_number = adapter_down_weight.shape[0]
    own_features = lax.dynamic_slice_in_dim(
        normed_input, head_index * feature_number, feature_number, 1
    )
    partial_every_token = jnp.dot(own_features, shrink_all, preferred_element_type=jnp.float32)
    partial_every_token = partial_every_token.reshape(
        token_device_rows, adapter_count, ADAPTER_RANK
    )
    pick = tok_adapter[:, None] == jnp.arange(adapter_count, dtype=jnp.int32)[None, :]
    partial_sum = jnp.sum(jnp.where(pick[:, :, None], partial_every_token, 0.0), axis=1)
    shrunk = lax.psum(partial_sum, "head").astype(jnp.bfloat16)
    spread_heads = jnp.where(pick[:, :, None], shrunk[:, None, :], jnp.zeros((), jnp.bfloat16))
    spread_heads = spread_heads.reshape(token_device_rows, adapter_count * ADAPTER_RANK)
    adapter_delta = jnp.dot(spread_heads, expand_every_token, preferred_element_type=jnp.float32)
    local_head_count = q_cols // HEAD_WIDTH
    queries = apply_rotation(
        (base_query + adapter_delta).reshape(token_device_rows, local_head_count, HEAD_WIDTH),
        token_position,
        HEAD_WIDTH,
    ).astype(jnp.bfloat16)
    kv_width = key_value_cache.shape[2]
    kv_heads = kv_width // HEAD_WIDTH
    page_count = logical_page_table.shape[1]
    paged = key_value_cache.reshape(page_count, token_device_rows // page_count, 2, kv_width)
    own_block = jnp.take(paged, logical_page_table[0], axis=0).reshape(
        token_device_rows, 2, kv_width
    )

    def pass_on(moving, unused):
        moved = from_behind(moving, "page", 1)
        return (moved, moved)

    unused_last, earlier = lax.scan(pass_on, own_block, None, length=span_count)
    stacked = jnp.concatenate([earlier[::-1], own_block[None]], axis=0)
    block_count = span_count + 1
    key_total = block_count * token_device_rows
    key_index = (page_index - span_count) * token_device_rows + jnp.arange(
        key_total, dtype=jnp.int32
    )
    visible = (key_index[None, :] >= tok_start[:, None]) & (key_index[None, :] <= token[:, None])
    inv_scale = 1.0 / math.sqrt(HEAD_WIDTH)
    group = local_head_count // kv_heads
    outputs = []
    for kv_head in range(kv_heads):
        low = kv_head * HEAD_WIDTH
        key_stack = stacked[:, :, 0, low : low + HEAD_WIDTH]
        value_stack = stacked[:, :, 1, low : low + HEAD_WIDTH]
        for member_head in range(group):
            query = queries[:, kv_head * group + member_head]
            keys_joined = key_stack.reshape(key_total, HEAD_WIDTH)
            values_joined = value_stack.reshape(key_total, HEAD_WIDTH)
            weights = normalize(score_block(query, keys_joined), visible, inv_scale)
            outputs.append(mix_block(weights, values_joined))
    attended = jnp.stack(outputs, axis=1).reshape(token_device_rows, q_cols).astype(jnp.bfloat16)
    return (queries.reshape(token_device_rows, q_cols), attended)


PAIR = 4


def swap(value, bit):
    count = lax.axis_size("page")
    return lax.ppermute(value, "page", [(p, p ^ bit) for p in range(count)])


def shift_z(value, steps):
    count = lax.axis_size("page")
    return lax.ppermute(value, "page", [(p, (p + 8 * steps) % count) for p in range(count)])


def in_order(flag, one, other):
    return jnp.where(
        flag == 0,
        jnp.concatenate([one, other], axis=0),
        jnp.concatenate([other, one], axis=0),
    )


def project_kernel(blocks, offsets, *refs):
    normed_refs, refs = refs[:PAIR], refs[PAIR:]
    weight_refs, refs = refs[:blocks], refs[blocks:]
    spread_ref, up_ref, cosine_ref, sine_ref, out_ref, held, sems = refs
    copies = [
        pltpu.make_async_copy(normed_refs[i], held.at[i], sems.at[i]) for i in range(PAIR)
    ]
    for copy in copies:
        copy.start()
    depth = weight_refs[0].shape[0]
    width = out_ref.shape[2]
    for i in range(PAIR):
        copies[i].wait()
        total = jnp.dot(spread_ref[i], up_ref[...], preferred_element_type=jnp.float32)
        for b in range(blocks):
            columns = pl.ds(pl.multiple_of(offsets[b], depth), depth)
            total += jnp.dot(
                held[i, :, columns], weight_refs[b][...], preferred_element_type=jnp.float32
            )
        cosine = cosine_ref[i]
        sine = sine_ref[i]
        for low in range(0, width, HEAD_WIDTH):
            head = total[:, low : low + HEAD_WIDTH]
            turned = head * cosine + pltpu.roll(head, HEAD_WIDTH // 2, 1) * sine
            out_ref[i, :, low : low + HEAD_WIDTH] = turned.astype(jnp.bfloat16)


def project(offsets, normed, weights, spread, up, cosine, sine):
    rows, features = normed[0].shape
    depth, width = weights[0].shape
    blocks = len(weights)
    vmem = pl.BlockSpec(memory_space=pltpu.VMEM)
    return pl.pallas_call(
        functools.partial(project_kernel, blocks),
        out_shape=jax.ShapeDtypeStruct((PAIR, rows, width), jnp.bfloat16),
        in_specs=[pl.BlockSpec(memory_space=pltpu.SMEM)]
        + [pl.BlockSpec(memory_space=pl.ANY)] * PAIR
        + [vmem] * (blocks + 4),
        out_specs=vmem,
        scratch_shapes=[
            pltpu.VMEM((PAIR, rows, features), jnp.bfloat16),
            pltpu.SemaphoreType.DMA((PAIR,)),
        ],
        compiler_params=pltpu.CompilerParams(vmem_limit_bytes=48 * 1024 * 1024),
        cost_estimate=pl.CostEstimate(
            flops=2 * PAIR * rows * features * width,
            bytes_accessed=2 * (PAIR * rows * features + features * width),
            transcendentals=0,
        ),
        name="project",
    )(offsets, *normed, *weights, spread, up, cosine, sine)


def attend_kernel(
    column,
    numbers,
    start_ref,
    query_ref,
    older_ref,
    old_ref,
    own_ref,
    out_ref,
    keys,
    values,
    turned,
    total,
    top_ref,
    sum_ref,
    sems,
):
    step = pl.program_id(0)
    tiles = pl.num_programs(0)
    rows = own_ref.shape[0] // PAIR
    group = query_ref.shape[2] // HEAD_WIDTH
    value_column = own_ref.shape[1] // 2 + column

    @pl.when(step == 0)
    def _():
        copies = []
        for b, source in enumerate((older_ref, old_ref, own_ref)):
            for i in range(PAIR):
                place = pl.multiple_of(numbers[4 * tiles + i] + b * PAIR * rows, rows)
                part = pl.ds(i * rows, rows)
                for kind, (low, target) in enumerate(((column, keys), (value_column, values))):
                    copies.append(
                        pltpu.make_async_copy(
                            source.at[part, pl.ds(low, HEAD_WIDTH)],
                            target.at[pl.ds(place, rows)],
                            sems.at[kind, b * PAIR + i],
                        )
                    )
        for copy in copies:
            copy.start()
        for copy in copies:
            copy.wait()

        def turn(i, carry):
            low = pl.multiple_of(i * KEY_TILE, KEY_TILE)
            part = values[pl.ds(low, KEY_TILE)].astype(jnp.float32)
            turned[:, pl.ds(low, KEY_TILE)] = part.T.astype(jnp.bfloat16)
            return carry

        lax.fori_loop(0, keys.shape[0] // KEY_TILE, turn, 0)

    first_token = numbers[step]
    low_start = numbers[tiles + step]
    high_start = numbers[2 * tiles + step]
    base = numbers[4 * tiles + PAIR]
    query = jnp.concatenate(
        [query_ref[0, :, h * HEAD_WIDTH : (h + 1) * HEAD_WIDTH] for h in range(group)], axis=0
    )
    factor = math.log2(math.e) / math.sqrt(HEAD_WIDTH)
    top_ref[...] = jnp.full(top_ref.shape, LOWEST, jnp.float32)
    sum_ref[...] = jnp.zeros(sum_ref.shape, jnp.float32)
    total[...] = jnp.zeros(total.shape, jnp.float32)

    def add(tile, masked):
        low = pl.multiple_of(tile * KEY_TILE, KEY_TILE)
        scores = lax.dot_general(
            keys[pl.ds(low, KEY_TILE)],
            query,
            (((1,), (1,)), ((), ())),
            preferred_element_type=jnp.float32,
        )
        scores = scores * factor
        if masked:
            shape = (KEY_TILE, TOKEN_TILE)
            key_index = base + low + lax.broadcasted_iota(jnp.int32, shape, 0)
            token = first_token + lax.broadcasted_iota(jnp.int32, shape, 1)
            seen = (key_index <= token) & (key_index >= start_ref[0])
            scores = jnp.concatenate(
                [
                    jnp.where(seen, scores[:, h * TOKEN_TILE : (h + 1) * TOKEN_TILE], LOWEST)
                    for h in range(group)
                ],
                axis=1,
            )
        old_top = top_ref[...]
        new_top = jnp.maximum(old_top, jnp.max(scores, axis=0, keepdims=True))
        expo = jnp.exp2(scores - new_top)
        shrink = jnp.exp2(old_top - new_top)
        top_ref[...] = new_top
        sum_ref[...] = sum_ref[...] * shrink + jnp.sum(expo, axis=0, keepdims=True)
        total[...] = total[...] * shrink + jnp.dot(
            turned[:, pl.ds(low, KEY_TILE)],
            expo.astype(jnp.bfloat16),
            preferred_element_type=jnp.float32,
        )

    def one_tile(tile, carry):
        low = base + tile * KEY_TILE
        whole = (low >= high_start) & (low + KEY_TILE - 1 <= first_token)

        @pl.when(whole)
        def _():
            add(tile, False)

        @pl.when(jnp.logical_not(whole))
        def _():
            add(tile, True)

        return carry

    from_tile = (low_start - base) // KEY_TILE
    to_tile = (first_token + TOKEN_TILE - 1 - base) // KEY_TILE + 1
    lax.fori_loop(from_tile, to_tile, one_tile, 0)
    mixed = total[...] / sum_ref[...]
    for h in range(group):
        part = mixed[:, h * TOKEN_TILE : (h + 1) * TOKEN_TILE]
        out_ref[0, :, h * HEAD_WIDTH : (h + 1) * HEAD_WIDTH] = part.T.astype(jnp.bfloat16)


def attend(column, numbers, tile_starts, queries, older, old, own):
    tiles, _, width = queries.shape
    key_total = 3 * own.shape[0]
    group = width // HEAD_WIDTH
    anywhere = pl.BlockSpec(memory_space=pl.ANY)
    return pl.pallas_call(
        functools.partial(attend_kernel, column),
        grid_spec=pltpu.PrefetchScalarGridSpec(
            num_scalar_prefetch=1,
            grid=(tiles,),
            in_specs=[
                pl.BlockSpec((1, 1, TOKEN_TILE), lambda i, n: (i, 0, 0)),
                pl.BlockSpec((1, TOKEN_TILE, width), lambda i, n: (i, 0, 0)),
                anywhere,
                anywhere,
                anywhere,
            ],
            out_specs=pl.BlockSpec((1, TOKEN_TILE, width), lambda i, n: (i, 0, 0)),
            scratch_shapes=[
                pltpu.VMEM((key_total, HEAD_WIDTH), jnp.bfloat16),
                pltpu.VMEM((key_total, HEAD_WIDTH), jnp.bfloat16),
                pltpu.VMEM((HEAD_WIDTH, key_total), jnp.bfloat16),
                pltpu.VMEM((HEAD_WIDTH, group * TOKEN_TILE), jnp.float32),
                pltpu.VMEM((1, group * TOKEN_TILE), jnp.float32),
                pltpu.VMEM((1, group * TOKEN_TILE), jnp.float32),
                pltpu.SemaphoreType.DMA((2, 3 * PAIR)),
            ],
        ),
        out_shape=jax.ShapeDtypeStruct(queries.shape, jnp.bfloat16),
        compiler_params=pltpu.CompilerParams(vmem_limit_bytes=48 * 1024 * 1024),
        cost_estimate=pl.CostEstimate(
            flops=4 * tiles * TOKEN_TILE * width * 2560,
            bytes_accessed=4 * tiles * TOKEN_TILE * width + 4 * key_total * HEAD_WIDTH,
            transcendentals=tiles * TOKEN_TILE * group * 2560,
        ),
        name="attend",
    )(numbers, tile_starts, queries, older, old, own)


def pair_body(
    hidden,
    attention_norm_gain,
    wq,
    adapter_down_weight,
    adapter_up_weight,
    key_value_cache,
    logical_page_table,
    lengths,
    prompt_adapter_index,
):
    rows, features = hidden.shape
    count = lax.axis_size("page")
    pairs = count // PAIR
    me = lax.axis_index("page")
    core, x, y, z = me % 2, (me // 2) % 2, (me // 4) % 2, me // 8
    pair = me // PAIR
    quarter = me % PAIR
    q_cols = wq.shape[1]
    width = q_cols // PAIR
    kv_width = key_value_cache.shape[2]
    kv_part = kv_width // PAIR
    kv_heads = kv_part // HEAD_WIDTH
    chunk = width // kv_heads

    def weight_part(part_x, part_core):
        return lax.dynamic_slice_in_dim(wq, (2 * part_x + part_core) * width, width, 1)

    from_core = swap(
        jnp.concatenate([weight_part(x, 1 - core), weight_part(1 - x, 1 - core)], axis=0), 1
    )
    wq_rows = wq.shape[0]
    from_x = swap(in_order(core, weight_part(1 - x, core), from_core[wq_rows:]), 2)
    weight_own = in_order(x, in_order(core, weight_part(x, core), from_core[:wq_rows]), from_x)

    page_count = logical_page_table.shape[1]
    paged = key_value_cache.reshape(page_count, rows // page_count, 2, kv_width)
    ordered = jnp.take(paged, logical_page_table[0], axis=0).reshape(rows, 2 * kv_width)

    def cache_part(part_x, part_core):
        low = (2 * part_x + part_core) * kv_part
        return jnp.concatenate(
            [
                lax.dynamic_slice_in_dim(ordered, low, kv_part, 1),
                lax.dynamic_slice_in_dim(ordered, kv_width + low, kv_part, 1),
            ],
            axis=1,
        )

    cache_core = swap(
        jnp.concatenate([cache_part(x, 1 - core), cache_part(1 - x, 1 - core)], axis=0), 1
    )
    cache_x = swap(jnp.concatenate([cache_part(1 - x, core), cache_core[rows:]], axis=0), 2)
    cache_own = jnp.concatenate([cache_part(x, core), cache_core[:rows], cache_x], axis=0)
    cache_older = lax.ppermute(cache_own, "page", [(p, p + 8) for p in range(count - 8)])
    cache_old = swap(jnp.where(y == 1, cache_older, cache_own), 4)

    wide = hidden.astype(jnp.float32)
    scale_rows = lax.rsqrt(jnp.mean(wide * wide, axis=-1, keepdims=True) + EPSILON)
    normed_own = (wide * scale_rows * attention_norm_gain.astype(jnp.float32)).astype(jnp.bfloat16)
    normed_core = swap(normed_own, 1)
    normed_x = swap(normed_own, 2)
    normed = [normed_own, normed_core, normed_x, swap(normed_x, 1)]

    ends = jnp.cumsum(lengths)
    starts = ends - lengths
    members = jnp.arange(PAIR, dtype=jnp.int32)
    block_device = pair * PAIR + (quarter ^ members)
    token = (block_device[:, None] * rows + jnp.arange(rows, dtype=jnp.int32)[None, :]).reshape(-1)
    member = (token[None, :] >= starts[:, None]) & (token[None, :] < ends[:, None])
    tok_start = jnp.sum(jnp.where(member, starts[:, None], 0), axis=0)
    position = (token - tok_start).astype(jnp.float32)
    half = HEAD_WIDTH // 2
    inverse = ROPE_BASE ** (-(jnp.arange(half, dtype=jnp.float32) * 2.0 / HEAD_WIDTH))
    angle = position[:, None] * inverse[None, :]
    cosine, sine = jnp.cos(angle), jnp.sin(angle)
    cosine = jnp.concatenate([cosine, cosine], axis=1).reshape(PAIR, rows, HEAD_WIDTH)
    sine = jnp.concatenate([-sine, sine], axis=1).reshape(PAIR, rows, HEAD_WIDTH)

    rank = adapter_up_weight.shape[0]
    slots = prompt_adapter_index.shape[0]
    part = width // pairs
    both = jnp.concatenate([adapter_down_weight.T, adapter_up_weight], axis=0)
    both = both.reshape(2 * rank, PAIR, pairs, part).transpose(2, 1, 0, 3)
    both = both.reshape(count * 2 * rank, part)
    every = lax.all_to_all(both, "page", split_axis=0, concat_axis=0, tiled=True)
    chosen = jnp.take(every.reshape(count, 2 * rank, part), prompt_adapter_index, axis=0)
    shared = lax.all_gather(
        chosen.reshape(slots * 2 * rank, part),
        "page",
        axis=0,
        tiled=False,
        axis_index_groups=[[q + PAIR * p for p in range(pairs)] for q in range(PAIR)],
    )
    shared = shared.reshape(pairs, slots, 2, rank, part).transpose(2, 1, 3, 0, 4)
    down = shared[0].reshape(slots * rank, width)
    up = shared[1].reshape(slots * rank, width)
    partial = []
    for i in range(PAIR):
        own_features = lax.dynamic_slice_in_dim(normed[i], quarter * width, width, 1)
        partial.append(
            lax.dot_general(
                down, own_features, (((1,), (1,)), ((), ())), preferred_element_type=jnp.float32
            )
        )
    partial = jnp.concatenate(partial, axis=1).reshape(slots, rank, PAIR * rows)
    partial = jnp.sum(jnp.where(member[:, None, :], partial, 0.0), axis=0)

    def moved(value, bit):
        got = swap(value, bit).reshape(rank, PAIR, rows)
        return jnp.stack([got[:, i ^ bit] for i in range(PAIR)], axis=1).reshape(value.shape)

    partial = partial + moved(partial, 1)
    partial = partial + moved(partial, 2)
    shrunk = partial.astype(jnp.bfloat16)
    spread = jnp.where(member[:, None, :], shrunk[None], jnp.zeros((), jnp.bfloat16))
    spread = spread.reshape(slots * rank, PAIR, rows).transpose(1, 2, 0)

    tiles = PAIR * rows // TOKEN_TILE
    tile_tokens = token.reshape(tiles, TOKEN_TILE)
    tile_starts = tok_start.reshape(tiles, TOKEN_TILE)
    numbers = jnp.concatenate(
        [
            tile_tokens[:, 0],
            tile_starts[:, 0],
            tile_starts[:, -1],
            jnp.zeros((tiles,), jnp.int32),
            (quarter ^ members) * rows,
            (pair * PAIR * rows - 2 * PAIR * rows)[None],
        ]
    ).astype(jnp.int32)
    tile_starts = tile_starts.reshape(tiles, 1, TOKEN_TILE)

    z_count = count // 8
    order = [0, 1, z_count - 1] + list(range(2, z_count - 1))
    offsets = jnp.stack(
        [
            ((((z - k) % z_count) * 2 + (y ^ dy)) * PAIR * wq_rows)
            for k in order
            for dy in (0, 1)
        ]
    ).astype(jnp.int32)
    results = []
    for g in range(kv_heads):
        piece = weight_own[:, g * chunk : (g + 1) * chunk]
        weights = []
        for k in order:
            along = shift_z(piece, k) if k else piece
            weights += [along, swap(along, 4)]
        queries = project(
            offsets, normed, weights, spread, up[:, g * chunk : (g + 1) * chunk], cosine, sine
        )
        attended = attend(
            g * HEAD_WIDTH,
            numbers,
            tile_starts,
            queries.reshape(tiles, TOKEN_TILE, chunk),
            cache_older,
            cache_old,
            cache_own,
        ).reshape(PAIR, rows, chunk)
        results.append((queries, attended))

    def home(value, g, whole):
        from_x = swap(value[2:], 2)
        from_core = swap(jnp.stack([value[1], from_x[1]]), 1)
        pieces = (
            (0, value[0]),
            (2, from_x[0]),
            (1, from_core[0]),
            (3, from_core[1]),
        )
        for bits, found in pieces:
            low = (quarter ^ bits) * width + g * chunk
            whole = lax.dynamic_update_slice_in_dim(whole, found, low, 1)
        return whole

    outs = []
    for kind in range(2):
        whole = jnp.zeros((rows, q_cols), jnp.bfloat16)
        for g in range(kv_heads):
            whole = home(results[g][kind], g, whole)
        outs.append(whole)
    return tuple(outs)


def solution(mesh):
    page, head = mesh.shape["page"], mesh.shape["head"]
    return jax.shard_map(
        pair_body if head == 1 and page == 32 else body,
        mesh=mesh,
        in_specs=(
            P("page", None),
            P(),
            P("page", "head"),
            P("head", "page"),
            P("page", "head"),
            P("page", None, "head"),
            P("page", None),
            P(),
            P(),
        ),
        out_specs=(P("page", "head"), P("page", "head")),
        check_vma=False,
    )
```

```python
import functools
import math

import jax
import jax.numpy as jnp
from jax import lax
from jax.experimental import pallas as pl
from jax.experimental.pallas import tpu as pltpu
from jax.sharding import PartitionSpec as P

HEAD_WIDTH = 128
ADAPTER_RANK = 16


EPSILON = 1e-05
ROPE_BASE = 500000.0
KEY_TILE = 512
LOWEST = -1e30


def from_behind(value, axis, steps):
    count = lax.axis_size(axis)
    leading, last = (max(0, -steps), min(count, count - steps))
    return lax.ppermute(value, axis, [(source, source + steps) for source in range(leading, last)])


def apply_rotation(values_f, token_position, head_size):
    half = head_size // 2
    inverse = ROPE_BASE ** (-(jnp.arange(half, dtype=jnp.float32) * 2.0 / head_size))
    angle = token_position.astype(jnp.float32)[:, None] * inverse[None, :]
    cosine = jnp.cos(angle)[:, None, :]
    sine = jnp.sin(angle)[:, None, :]
    first = values_f[..., :half]
    second = values_f[..., half:]
    return jnp.concatenate(
        [first * cosine - second * sine, second * cosine + first * sine], axis=-1
    )


def score_block(query, keyblock):
    return lax.dot_general(
        query, keyblock, (((1,), (1,)), ((), ())), preferred_element_type=jnp.float32
    )


def mix_block(weights, valueblock):
    return jnp.dot(weights, valueblock, preferred_element_type=jnp.float32)


def normalize(scores, visible, inv_scale):
    scores = jnp.where(visible, scores * inv_scale, -jnp.inf)
    top = jnp.max(scores, axis=-1, keepdims=True)
    expo = jnp.exp(scores - top)
    return (expo / jnp.sum(expo, axis=-1, keepdims=True)).astype(jnp.bfloat16)


def body(
    hidden,
    attention_norm_gain,
    wq,
    adapter_down_weight,
    adapter_up_weight,
    key_value_cache,
    logical_page_table,
    lengths,
    prompt_adapter_index,
):
    token_device_rows = hidden.shape[0]
    page_index = lax.axis_index("page")
    head_index = lax.axis_index("head")
    span_count = lax.axis_size("page") // 4
    x = hidden.astype(jnp.float32)
    scale_rows = lax.rsqrt(jnp.mean(x * x, axis=-1, keepdims=True) + EPSILON)
    normed_input = (x * scale_rows * attention_norm_gain.astype(jnp.float32)).astype(jnp.bfloat16)
    ends = jnp.cumsum(lengths)
    starts = ends - lengths
    token = page_index * token_device_rows + jnp.arange(token_device_rows, dtype=jnp.int32)
    member = (token[:, None] >= starts[None, :]) & (token[:, None] < ends[None, :])
    tok_start = jnp.sum(jnp.where(member, starts[None, :], 0), axis=1)
    tok_adapter = jnp.sum(jnp.where(member, prompt_adapter_index[None, :], 0), axis=1)
    token_position = token - tok_start
    q_cols = wq.shape[1]
    base_query = jnp.dot(
        normed_input,
        lax.all_gather(wq, "page", axis=0, tiled=True),
        preferred_element_type=jnp.float32,
    )
    shrink_all, expand_every_token = (
        lax.all_gather(adapter_down_weight, "page", axis=1, tiled=True),
        lax.all_gather(adapter_up_weight, "page", axis=0, tiled=True),
    )
    adapter_count = shrink_all.shape[1] // ADAPTER_RANK
    feature_number = adapter_down_weight.shape[0]
    own_features = lax.dynamic_slice_in_dim(
        normed_input, head_index * feature_number, feature_number, 1
    )
    partial_every_token = jnp.dot(own_features, shrink_all, preferred_element_type=jnp.float32)
    partial_every_token = partial_every_token.reshape(
        token_device_rows, adapter_count, ADAPTER_RANK
    )
    pick = tok_adapter[:, None] == jnp.arange(adapter_count, dtype=jnp.int32)[None, :]
    partial_sum = jnp.sum(jnp.where(pick[:, :, None], partial_every_token, 0.0), axis=1)
    shrunk = lax.psum(partial_sum, "head").astype(jnp.bfloat16)
    spread_heads = jnp.where(pick[:, :, None], shrunk[:, None, :], jnp.zeros((), jnp.bfloat16))
    spread_heads = spread_heads.reshape(token_device_rows, adapter_count * ADAPTER_RANK)
    adapter_delta = jnp.dot(spread_heads, expand_every_token, preferred_element_type=jnp.float32)
    local_head_count = q_cols // HEAD_WIDTH
    queries = apply_rotation(
        (base_query + adapter_delta).reshape(token_device_rows, local_head_count, HEAD_WIDTH),
        token_position,
        HEAD_WIDTH,
    ).astype(jnp.bfloat16)
    kv_width = key_value_cache.shape[2]
    kv_heads = kv_width // HEAD_WIDTH
    page_count = logical_page_table.shape[1]
    paged = key_value_cache.reshape(page_count, token_device_rows // page_count, 2, kv_width)
    own_block = jnp.take(paged, logical_page_table[0], axis=0).reshape(
        token_device_rows, 2, kv_width
    )

    def pass_on(moving, unused):
        moved = from_behind(moving, "page", 1)
        return (moved, moved)

    unused_last, earlier = lax.scan(pass_on, own_block, None, length=span_count)
    stacked = jnp.concatenate([earlier[::-1], own_block[None]], axis=0)
    block_count = span_count + 1
    key_total = block_count * token_device_rows
    key_index = (page_index - span_count) * token_device_rows + jnp.arange(
        key_total, dtype=jnp.int32
    )
    visible = (key_index[None, :] >= tok_start[:, None]) & (key_index[None, :] <= token[:, None])
    inv_scale = 1.0 / math.sqrt(HEAD_WIDTH)
    group = local_head_count // kv_heads
    outputs = []
    for kv_head in range(kv_heads):
        low = kv_head * HEAD_WIDTH
        key_stack = stacked[:, :, 0, low : low + HEAD_WIDTH]
        value_stack = stacked[:, :, 1, low : low + HEAD_WIDTH]
        for member_head in range(group):
            query = queries[:, kv_head * group + member_head]
            keys_joined = key_stack.reshape(key_total, HEAD_WIDTH)
            values_joined = value_stack.reshape(key_total, HEAD_WIDTH)
            weights = normalize(score_block(query, keys_joined), visible, inv_scale)
            outputs.append(mix_block(weights, values_joined))
    attended = jnp.stack(outputs, axis=1).reshape(token_device_rows, q_cols).astype(jnp.bfloat16)
    return (queries.reshape(token_device_rows, q_cols), attended)


PAIR = 4


def swap(value, bit):
    count = lax.axis_size("page")
    return lax.ppermute(value, "page", [(p, p ^ bit) for p in range(count)])


def shift_z(value, steps):
    count = lax.axis_size("page")
    return lax.ppermute(value, "page", [(p, (p + 8 * steps) % count) for p in range(count)])


class Transfers:
    def __init__(self):
        self.found = {}

    def __getitem__(self, name):
        return self.found[name]

    def tie(self, values, waits):
        waits = list(waits)
        tied = lax.optimization_barrier((*values, *[self.found[name] for name in waits]))
        for name, value in zip(waits, tied[len(values) :]):
            self.found[name] = value
        return list(tied[: len(values)])

    def run(self, waits, sends):
        operands = [operand for _, operand, _ in sends]
        if waits:
            operands = self.tie(operands, waits)
        for (name, _, move), operand in zip(sends, operands):
            self.found[name] = move(operand)


def in_order(flag, one, other):
    return jnp.where(
        flag == 0,
        jnp.concatenate([one, other], axis=0),
        jnp.concatenate([other, one], axis=0),
    )


def member_rows(value, first_token, starts, ends):
    token = first_token + lax.broadcasted_iota(jnp.int32, (1, value.shape[1]), 1)
    return [
        jnp.where((token >= start) & (token < end), value, 0.0) for start, end in zip(starts, ends)
    ]


def choose_kernel(which, every_ref, out_ref, held, sems):
    slots = which.shape[0]
    rank = every_ref.shape[1] // 2
    copies = []
    for r in range(slots):
        for kind in range(2):
            copies.append(
                pltpu.make_async_copy(
                    every_ref.at[which[r], pl.ds(kind * rank, rank)],
                    held.at[pl.ds((kind * slots + r) * rank, rank)],
                    sems.at[kind, r],
                )
            )
    for copy in copies:
        copy.start()
    for copy in copies:
        copy.wait()
    rows, width = out_ref.shape
    part = held.shape[1]
    for h in range(width // part):
        out_ref[:, h * part : (h + 1) * part] = held[h * rows : (h + 1) * rows]


def choose(which, every, width):
    slots = which.shape[0]
    _, rows, part = every.shape
    return pl.pallas_call(
        choose_kernel,
        out_shape=jax.ShapeDtypeStruct((slots * rows * part // width, width), every.dtype),
        in_specs=[pl.BlockSpec(memory_space=pltpu.SMEM), pl.BlockSpec(memory_space=pl.ANY)],
        out_specs=pl.BlockSpec(memory_space=pltpu.VMEM),
        scratch_shapes=[
            pltpu.VMEM((slots * rows, part), every.dtype),
            pltpu.SemaphoreType.DMA((2, slots)),
        ],
        cost_estimate=pl.CostEstimate(flops=1000, bytes_accessed=1000, transcendentals=0),
        name="choose",
    )(which, every)


def shrink_kernel(layout, blocks, depth, part, numbers, *refs):
    normed_refs, refs = refs[: len(layout)], refs[len(layout) :]
    weight_refs, refs = refs[:blocks], refs[blocks:]
    out_ref, up_ref, held, adapters, normed_sems, sems = refs
    rank, columns = out_ref.shape
    rows = columns // PAIR
    features = held.shape[2]
    slots = adapters.shape[0] // (2 * rank)
    extra = weight_refs[0].shape[0] - depth
    quarter = numbers[0]
    columns_here = pl.ds(pl.multiple_of(quarter * features, features), features)
    copies = [
        pltpu.make_async_copy(
            ref.at[:, columns_here], held.at[i, pl.ds(low, ref.shape[0])], normed_sems.at[n]
        )
        for n, (ref, (i, low)) in enumerate(zip(normed_refs, layout))
    ]
    for b in range(blocks):
        place = pl.multiple_of(numbers[1 + b] * part, part)
        for h in range(2 * slots * rank // extra):
            copies.append(
                pltpu.make_async_copy(
                    weight_refs[b].at[pl.ds(depth, extra), pl.ds(h * part, part)],
                    adapters.at[pl.ds(h * extra, extra), pl.ds(place, part)],
                    sems.at[b, h],
                )
            )
    for copy in copies:
        copy.start()
    for copy in copies:
        copy.wait()
    up_ref[...] = adapters[slots * rank :]
    at = 1 + blocks + PAIR
    starts = [numbers[at + r] for r in range(slots)]
    ends = [numbers[at + slots + r] for r in range(slots)]
    for i in range(PAIR):
        partial = lax.dot_general(
            adapters[: slots * rank],
            held[i],
            (((1,), (1,)), ((), ())),
            preferred_element_type=jnp.float32,
        )
        token = numbers[1 + blocks + i] + lax.broadcasted_iota(jnp.int32, (1, rows), 1)
        found = jnp.zeros((rank, rows), jnp.float32)
        for r in range(slots):
            member = (token >= starts[r]) & (token < ends[r])
            found += jnp.where(member, partial[r * rank : (r + 1) * rank], 0.0)
        place = pl.multiple_of((quarter ^ i) * rows, HEAD_WIDTH)
        out_ref[:, pl.ds(place, rows)] = found


def shrink(numbers, layout, normed, weights, depth, part, slots, rank):
    rows, _ = normed[0].shape
    blocks = len(weights)
    extra, width = weights[0].shape[0] - depth, blocks * part
    vmem = pl.BlockSpec(memory_space=pltpu.VMEM)
    return pl.pallas_call(
        functools.partial(shrink_kernel, layout, blocks, depth, part),
        out_shape=(
            jax.ShapeDtypeStruct((rank, PAIR * rows), jnp.float32),
            jax.ShapeDtypeStruct((slots * rank, width), jnp.bfloat16),
        ),
        in_specs=[pl.BlockSpec(memory_space=pltpu.SMEM)]
        + [pl.BlockSpec(memory_space=pl.ANY)] * (len(layout) + blocks),
        out_specs=(vmem, vmem),
        scratch_shapes=[
            pltpu.VMEM((PAIR, rows, width), jnp.bfloat16),
            pltpu.VMEM((2 * slots * rank, width), jnp.bfloat16),
            pltpu.SemaphoreType.DMA((len(layout),)),
            pltpu.SemaphoreType.DMA((blocks, 2 * slots * rank // extra)),
        ],
        compiler_params=pltpu.CompilerParams(vmem_limit_bytes=60 * 1024 * 1024),
        cost_estimate=pl.CostEstimate(flops=1000, bytes_accessed=1000, transcendentals=0),
        name="shrink",
    )(numbers, *normed, *weights)


def project_kernel(layout, blocks, numbers, *refs):
    normed_refs, refs = refs[: len(layout)], refs[len(layout) :]
    weight_refs, refs = refs[:blocks], refs[blocks:]
    shrunk_ref, up_ref, cosine_ref, sine_ref, out_ref, held, weight, sems = refs
    width = out_ref.shape[2]
    rows = out_ref.shape[1]
    depth = weight.shape[0] // blocks
    rank = shrunk_ref.shape[0]
    slots = up_ref.shape[0] // rank
    weight_copies = [
        pltpu.make_async_copy(
            weight_refs[b].at[pl.ds(0, depth)],
            weight.at[pl.ds(pl.multiple_of(numbers[1 + b] * depth, depth), depth)],
            sems.at[len(layout) + b],
        )
        for b in range(blocks)
    ]
    copies = [
        pltpu.make_async_copy(ref, held.at[i, pl.ds(low, ref.shape[0])], sems.at[n])
        for n, (ref, (i, low)) in enumerate(zip(normed_refs, layout))
    ]
    for copy in weight_copies + copies:
        copy.start()
    for copy in weight_copies:
        copy.wait()
    at = 1 + blocks + PAIR
    starts = [numbers[at + r] for r in range(slots)]
    ends = [numbers[at + slots + r] for r in range(slots)]
    for i in range(PAIR):
        for copy, (block, _) in zip(copies, layout):
            if block == i:
                copy.wait()
        block = numbers[0] ^ i
        place = pl.multiple_of(block * rows, HEAD_WIDTH)
        shrunk = shrunk_ref[:, pl.ds(place, rows)].astype(jnp.float32)
        spread = member_rows(shrunk, numbers[1 + blocks + i], starts, ends)
        spread = jnp.concatenate(spread, axis=0).astype(jnp.bfloat16)
        total = lax.dot_general(
            spread, up_ref[...], (((0,), (0,)), ((), ())), preferred_element_type=jnp.float32
        )
        total += jnp.dot(held[i], weight[...], preferred_element_type=jnp.float32)
        cosine = cosine_ref[block]
        sine = sine_ref[block]
        for low in range(0, width, HEAD_WIDTH):
            head = total[:, low : low + HEAD_WIDTH]
            turned = head * cosine + pltpu.roll(head, HEAD_WIDTH // 2, 1) * sine
            out_ref[block, :, low : low + HEAD_WIDTH] = turned.astype(jnp.bfloat16)


def project(numbers, layout, normed, weights, shrunk, up, cosine, sine):
    rows, features = normed[0].shape
    width = weights[0].shape[1]
    blocks = len(weights)
    vmem = pl.BlockSpec(memory_space=pltpu.VMEM)
    return pl.pallas_call(
        functools.partial(project_kernel, layout, blocks),
        out_shape=jax.ShapeDtypeStruct((PAIR, rows, width), jnp.bfloat16),
        in_specs=[pl.BlockSpec(memory_space=pltpu.SMEM)]
        + [pl.BlockSpec(memory_space=pl.ANY)] * (len(layout) + blocks)
        + [vmem] * 4,
        out_specs=vmem,
        scratch_shapes=[
            pltpu.VMEM((PAIR, rows, features), jnp.bfloat16),
            pltpu.VMEM((features, width), jnp.bfloat16),
            pltpu.SemaphoreType.DMA((len(layout) + blocks,)),
        ],
        compiler_params=pltpu.CompilerParams(vmem_limit_bytes=60 * 1024 * 1024),
        cost_estimate=pl.CostEstimate(flops=1000, bytes_accessed=1000, transcendentals=0),
        name="project",
    )(numbers, *normed, *weights, shrunk, up, cosine, sine)


def attend_kernel(
    column,
    numbers,
    start_ref,
    query_ref,
    older_ref,
    old_ref,
    own_ref,
    out_ref,
    keys,
    values,
    turned,
    total,
    top_ref,
    sems,
):
    step = pl.program_id(0)
    tiles = pl.num_programs(0)
    rows = own_ref.shape[0] // PAIR
    tile_rows = query_ref.shape[1]
    group = query_ref.shape[2] // HEAD_WIDTH
    value_column = own_ref.shape[1] // 2 + column

    @pl.when(step == 0)
    def _():
        copies = []
        for kind, (low, target) in enumerate(((value_column, values), (column, keys))):
            for b, source in enumerate((older_ref, old_ref, own_ref)):
                for i in range(PAIR):
                    place = pl.multiple_of(numbers[2 * tiles + i] + b * PAIR * rows, rows)
                    copies.append(
                        pltpu.make_async_copy(
                            source.at[pl.ds(i * rows, rows), pl.ds(low, HEAD_WIDTH)],
                            target.at[pl.ds(place, rows)],
                            sems.at[kind, b * PAIR + i],
                        )
                    )
        for copy in copies:
            copy.start()
        ones = turned.shape[0] - HEAD_WIDTH
        turned[HEAD_WIDTH:] = jnp.ones((ones, turned.shape[1]), jnp.bfloat16)
        for copy in copies[: len(copies) // 2]:
            copy.wait()

        def turn(i, carry):
            low = pl.multiple_of(i * KEY_TILE, KEY_TILE)
            turned[:HEAD_WIDTH, pl.ds(low, KEY_TILE)] = values[pl.ds(low, KEY_TILE)].T
            return carry

        lax.fori_loop(0, keys.shape[0] // KEY_TILE, turn, 0)
        for copy in copies[len(copies) // 2 :]:
            copy.wait()

    first_token = numbers[step]
    low_start = numbers[tiles + step]
    base = numbers[2 * tiles + PAIR]
    queries = [query_ref[0, :, h * HEAD_WIDTH : (h + 1) * HEAD_WIDTH] for h in range(group)]
    factor = math.log2(math.e) / math.sqrt(HEAD_WIDTH)
    top_ref[...] = jnp.full(top_ref.shape, LOWEST, jnp.float32)
    total[...] = jnp.zeros(total.shape, jnp.float32)

    def one_tile(tile, carry):
        low = pl.multiple_of(tile * KEY_TILE, KEY_TILE)
        shape = (KEY_TILE, tile_rows)
        key_index = base + low + lax.broadcasted_iota(jnp.int32, shape, 0)
        token = first_token + lax.broadcasted_iota(jnp.int32, shape, 1)
        seen = (key_index <= token) & (key_index >= start_ref[0])
        here = keys[pl.ds(low, KEY_TILE)]
        products = [
            lax.dot_general(
                here, query, (((1,), (1,)), ((), ())), preferred_element_type=jnp.float32
            )
            for query in queries
        ]
        for h in range(group):
            scores = jnp.where(seen, products[h] * factor, LOWEST)
            old_top = top_ref[h]
            new_top = jnp.maximum(old_top, jnp.max(scores, axis=0, keepdims=True))
            expo = jnp.exp2(scores - new_top)
            top_ref[h] = new_top
            total[h] = total[h] * jnp.exp2(old_top - new_top) + jnp.dot(
                turned[:, pl.ds(low, KEY_TILE)],
                expo.astype(jnp.bfloat16),
                preferred_element_type=jnp.float32,
            )
        return carry

    from_tile = (low_start - base) // KEY_TILE
    to_tile = (first_token + tile_rows - 1 - base) // KEY_TILE + 1
    lax.fori_loop(from_tile, to_tile, one_tile, 0)
    for h in range(group):
        mixed = total[h, :HEAD_WIDTH] / total[h, HEAD_WIDTH : HEAD_WIDTH + 1]
        out_ref[0, :, h * HEAD_WIDTH : (h + 1) * HEAD_WIDTH] = mixed.T.astype(jnp.bfloat16)


def attend(column, numbers, tile_starts, queries, older, old, own):
    tiles, tile_rows, width = queries.shape
    key_total = 3 * own.shape[0]
    group = width // HEAD_WIDTH
    deep = HEAD_WIDTH + 16
    anywhere = pl.BlockSpec(memory_space=pl.ANY)
    return pl.pallas_call(
        functools.partial(attend_kernel, column),
        grid_spec=pltpu.PrefetchScalarGridSpec(
            num_scalar_prefetch=1,
            grid=(tiles,),
            in_specs=[
                pl.BlockSpec((1, 1, tile_rows), lambda i, n: (i, 0, 0)),
                pl.BlockSpec((1, tile_rows, width), lambda i, n: (i, 0, 0)),
                anywhere,
                anywhere,
                anywhere,
            ],
            out_specs=pl.BlockSpec((1, tile_rows, width), lambda i, n: (i, 0, 0)),
            scratch_shapes=[
                pltpu.VMEM((key_total, HEAD_WIDTH), jnp.bfloat16),
                pltpu.VMEM((key_total, HEAD_WIDTH), jnp.bfloat16),
                pltpu.VMEM((deep, key_total), jnp.bfloat16),
                pltpu.VMEM((group, deep, tile_rows), jnp.float32),
                pltpu.VMEM((group, 1, tile_rows), jnp.float32),
                pltpu.SemaphoreType.DMA((2, 3 * PAIR)),
            ],
        ),
        out_shape=jax.ShapeDtypeStruct(queries.shape, jnp.bfloat16),
        compiler_params=pltpu.CompilerParams(vmem_limit_bytes=60 * 1024 * 1024),
        cost_estimate=pl.CostEstimate(flops=1000, bytes_accessed=1000, transcendentals=0),
        name="attend",
    )(numbers, tile_starts, queries, older, old, own)


def pair_body(
    hidden,
    attention_norm_gain,
    wq,
    adapter_down_weight,
    adapter_up_weight,
    key_value_cache,
    logical_page_table,
    lengths,
    prompt_adapter_index,
):
    rows, features = hidden.shape
    count = lax.axis_size("page")
    me = lax.axis_index("page")
    core, x, y, z = me % 2, (me // 2) % 2, (me // 4) % 2, me // 8
    pair = me // PAIR
    quarter = me % PAIR
    q_cols = wq.shape[1]
    width = q_cols // PAIR
    kv_width = key_value_cache.shape[2]
    kv_part = kv_width // PAIR
    kv_heads = kv_part // HEAD_WIDTH
    chunk = width // kv_heads

    def weight_part(part_x, part_core):
        return lax.dynamic_slice_in_dim(wq, (2 * part_x + part_core) * width, width, 1)

    sent = Transfers()
    core_swap = functools.partial(swap, bit=1)
    x_swap = functools.partial(swap, bit=2)
    y_swap = functools.partial(swap, bit=4)
    wq_rows = wq.shape[0]
    wq_depth = PAIR * wq_rows
    pairs = count // PAIR
    z_count = count // 8
    order = (0, 1, 3, 2)

    rank = adapter_up_weight.shape[0]
    slots = prompt_adapter_index.shape[0]
    part = width // pairs
    both = jnp.concatenate([adapter_down_weight.T, adapter_up_weight], axis=0)
    both = both.reshape(2 * rank, PAIR, pairs, part).transpose(2, 1, 0, 3)
    both = both.reshape(count * 2 * rank, part)

    def exchange(value):
        return lax.all_to_all(value, "page", split_axis=0, concat_axis=0, tiled=True)

    sent.run([], [("adapters", both, exchange)])
    sent.run(
        [],
        [
            (
                "weight c",
                jnp.concatenate([weight_part(x, 1 - core), weight_part(1 - x, 1 - core)], axis=0),
                core_swap,
            )
        ],
    )
    from_core = sent["weight c"]
    mine = in_order(core, weight_part(1 - x, core), from_core[wq_rows:])
    kept = in_order(core, weight_part(x, core), from_core[:wq_rows])
    sent.run([], [("weight x0", mine[:, :chunk], x_swap)])
    key_value_cache, hidden = sent.tie([key_value_cache, hidden], ["weight x0"])

    page_count = logical_page_table.shape[1]
    page_rows = rows // page_count
    paged = key_value_cache.reshape(page_count, page_rows, 2, kv_width)
    ordered = jnp.concatenate(
        [
            lax.dynamic_index_in_dim(paged, logical_page_table[0, j], 0, keepdims=False)
            for j in range(page_count)
        ],
        axis=0,
    ).reshape(rows, 2 * kv_width)

    def cache_part(part_x, part_core):
        low = (2 * part_x + part_core) * kv_part
        return jnp.concatenate(
            [
                lax.dynamic_slice_in_dim(ordered, low, kv_part, 1),
                lax.dynamic_slice_in_dim(ordered, kv_width + low, kv_part, 1),
            ],
            axis=1,
        )

    sent.run(
        [],
        [
            (
                "cache c",
                jnp.concatenate([cache_part(x, 1 - core), cache_part(1 - x, 1 - core)], axis=0),
                core_swap,
            )
        ],
    )
    cache_core = sent["cache c"]

    wide = hidden.astype(jnp.float32)
    scale_rows = lax.rsqrt(jnp.mean(wide * wide, axis=-1, keepdims=True) + EPSILON)
    normed_own = (wide * scale_rows * attention_norm_gain.astype(jnp.float32)).astype(jnp.bfloat16)
    half_rows = rows // 2
    ends = jnp.cumsum(lengths)
    starts = ends - lengths
    first_token = pair * (PAIR * rows)
    token = first_token + jnp.arange(PAIR * rows, dtype=jnp.int32)
    member = (token[None, :] >= starts[:, None]) & (token[None, :] < ends[:, None])
    tok_start = jnp.sum(jnp.where(member, starts[:, None], 0), axis=0)
    position = (token - tok_start).astype(jnp.float32)
    half = HEAD_WIDTH // 2
    inverse = ROPE_BASE ** (-(jnp.arange(half, dtype=jnp.float32) * 2.0 / HEAD_WIDTH))
    angle = position[:, None] * inverse[None, :]
    cosine, sine = jnp.cos(angle), jnp.sin(angle)
    cosine = jnp.concatenate([cosine, cosine], axis=1).reshape(PAIR, rows, HEAD_WIDTH)
    sine = jnp.concatenate([-sine, sine], axis=1).reshape(PAIR, rows, HEAD_WIDTH)

    chosen = choose(prompt_adapter_index, sent["adapters"].reshape(count, 2 * rank, part), chunk)
    pieces = [
        jnp.concatenate([in_order(x, kept[:, :chunk], sent["weight x0"]), chosen], axis=0)
    ]

    def along_z(g, k):
        return (f"z{g} {k}", pieces[g], functools.partial(shift_z, steps=k))

    def along_y(g, k):
        return (f"y{g} {k}", sent[f"z{g} {k}"] if k else pieces[g], y_swap)

    def older(value):
        return lax.ppermute(value, "page", [(p, p + 8) for p in range(count - 8)])

    cuts = (0, rows // 2, rows)

    def normed_part(n):
        return (f"normed x{n}", normed_own[cuts[n] : cuts[n + 1]], x_swap)

    def normed_on(n):
        return (f"normed xc{n}", sent[f"normed x{n}"], core_swap)

    sent.run(
        ["weight x0"],
        [
            along_z(0, 1),
            along_z(0, 3),
            along_y(0, 0),
            ("weight x1", mine[:, chunk:], x_swap),
        ],
    )
    sent.run(
        [],
        [
            ("normed c", normed_own, core_swap),
            (
                "cache x",
                jnp.concatenate([cache_part(1 - x, core), cache_core[rows:]], axis=0),
                x_swap,
            ),
        ],
    )
    pieces.append(in_order(x, kept[:, chunk:], sent["weight x1"]))
    sent.run(
        ["z0 1", "z0 3", "y0 0", "weight x1", "cache x", "normed c"],
        [
            along_z(0, 2),
            along_z(1, 1),
            along_y(0, 1),
            along_y(0, 3),
            along_y(1, 0),
            normed_part(0),
        ],
    )
    cache_own = jnp.concatenate([cache_part(x, core), cache_core[:rows], sent["cache x"]], axis=0)
    cosine, sine = sent.tie([cosine, sine], ["y0 1"])
    sent.run(
        ["z0 2", "z1 1", "y0 1", "y0 3", "y1 0", "normed x0"],
        [
            ("cache z", cache_own, older),
            along_y(0, 2),
            along_y(1, 1),
            normed_part(1),
            normed_on(0),
        ],
    )
    sent.run(
        ["cache z", "y0 2", "y1 1", "normed x1", "normed xc0"],
        [
            normed_on(1),
            along_z(1, 3),
            along_z(1, 2),
            ("cache y", jnp.where(y == 1, sent["cache z"], cache_own), y_swap),
        ],
    )
    normed = [normed_own, sent["normed c"]]
    normed += [sent[f"normed {way}{n}"] for way in ("x", "xc") for n in range(2)]
    layout = ((0, 0), (1, 0)) + tuple((i, cuts[n]) for i in (2, 3) for n in range(2))

    def weights_of(g):
        return [
            sent[f"{way}{g} {k}"] if k or way == "y" else pieces[g] for k in order for way in "zy"
        ]

    members = jnp.arange(PAIR, dtype=jnp.int32)
    places = [((z - k) % z_count) * 2 + (y ^ dy) for k in order for dy in (0, 1)]
    numbers = jnp.concatenate(
        [
            quarter[None],
            jnp.stack(places),
            first_token + (quarter ^ members) * rows,
            starts,
            ends,
        ]
    ).astype(jnp.int32)
    weights0 = weights_of(0)
    partial, up = shrink(numbers, layout, normed, weights0, wq_depth, part, slots, rank)
    partial = partial + swap(partial, 1)
    partial = partial + swap(partial, 2)
    shrunk = partial.astype(jnp.bfloat16)

    def project_part(g, weights, shrunk):
        return project(
            numbers, layout, normed, weights, shrunk, up[:, g * chunk : (g + 1) * chunk], cosine, sine
        )

    def attend_part(g, queries, from_row, tile_rows):
        count_rows = queries.shape[0] * queries.shape[1]
        tiles = count_rows // tile_rows
        here = lax.dynamic_slice_in_dim(tok_start, from_row, count_rows, 0)
        here = here.reshape(tiles, 1, tile_rows)
        steps = jnp.concatenate(
            [
                first_token + from_row + jnp.arange(tiles, dtype=jnp.int32) * tile_rows,
                here[:, 0, 0],
                (quarter ^ members) * rows,
                (first_token - 2 * PAIR * rows)[None],
            ]
        ).astype(jnp.int32)
        return attend(
            g * HEAD_WIDTH,
            steps,
            here,
            queries.reshape(tiles, tile_rows, chunk),
            sent["cache z"],
            sent["cache y"],
            cache_own,
        ).reshape(queries.shape)

    def away(value):
        return lax.dynamic_slice_in_dim(value, 2 * (1 - x), 2, 0)

    def at_home(value):
        return lax.dynamic_slice_in_dim(value, 2 * x, 2, 0)

    def home(stay, from_x, g, whole):

        def block(found, which):
            return lax.dynamic_index_in_dim(found, which, 0, keepdims=False)

        from_core = swap(jnp.stack([block(stay, 1 - core), block(from_x, 1 - core)]), 1)
        found = (
            (0, block(stay, core)),
            (2, block(from_x, core)),
            (1, from_core[0]),
            (3, from_core[1]),
        )
        for bits, piece in found:
            low = (quarter ^ bits) * width + g * chunk
            whole = lax.dynamic_update_slice_in_dim(whole, piece, low, 1)
        return whole

    queries0 = project_part(0, weights0, shrunk)
    sent.run(
        ["cache y", "z1 3", "z1 2"],
        [along_y(1, 3), along_y(1, 2), ("queries x0", away(queries0), x_swap)],
    )
    attended0 = attend_part(0, queries0, 0, PAIR * rows // 3)
    sent.run([], [("attended x0", away(attended0), x_swap)])
    (shrunk,) = sent.tie([shrunk], ["queries x0"])
    queries1 = project_part(1, weights_of(1), shrunk)
    queries_away = away(queries1)
    sent.run([], [("queries x1", queries_away, x_swap)])
    (queries_away,) = sent.tie([queries_away], ["attended x0"])
    attended_away = attend_part(1, queries_away, 2 * (1 - x) * rows, rows)
    sent.run([], [("attended x1", attended_away, x_swap)])
    (queries_home,) = sent.tie([at_home(queries1)], ["queries x1"])
    attended1 = attend_part(1, queries_home, 2 * x * rows, rows)
    outs = []
    for name, parts in (
        ("queries", (at_home(queries0), queries_home)),
        ("attended", (at_home(attended0), attended1)),
    ):
        whole = jnp.zeros((rows, q_cols), jnp.bfloat16)
        for g, stay in enumerate(parts):
            whole = home(stay, sent[f"{name} x{g}"], g, whole)
        outs.append(whole)
    return tuple(outs)


def solution(mesh):
    page, head = mesh.shape["page"], mesh.shape["head"]
    return jax.shard_map(
        pair_body if head == 1 and page == 32 else body,
        mesh=mesh,
        in_specs=(
            P("page", None),
            P(),
            P("page", "head"),
            P("head", "page"),
            P("page", "head"),
            P("page", None, "head"),
            P("page", None),
            P(),
            P(),
        ),
        out_specs=(P("page", "head"), P("page", "head")),
        check_vma=False,
    )
```

```python
import functools
import math

import jax
import jax.numpy as jnp
from jax import lax
from jax.experimental import pallas as pl
from jax.experimental.pallas import tpu as pltpu
from jax.sharding import PartitionSpec as P

HEAD_WIDTH = 128
ADAPTER_RANK = 16


EPSILON = 1e-05
ROPE_BASE = 500000.0
KEY_TILE = 512
LOWEST = -1e30
SAFE_POWER = 90.0


def from_behind(value, axis, steps):
    count = lax.axis_size(axis)
    leading, last = (max(0, -steps), min(count, count - steps))
    return lax.ppermute(value, axis, [(source, source + steps) for source in range(leading, last)])


def apply_rotation(values_f, token_position, head_size):
    half = head_size // 2
    inverse = ROPE_BASE ** (-(jnp.arange(half, dtype=jnp.float32) * 2.0 / head_size))
    angle = token_position.astype(jnp.float32)[:, None] * inverse[None, :]
    cosine = jnp.cos(angle)[:, None, :]
    sine = jnp.sin(angle)[:, None, :]
    first = values_f[..., :half]
    second = values_f[..., half:]
    return jnp.concatenate(
        [first * cosine - second * sine, second * cosine + first * sine], axis=-1
    )


def score_block(query, keyblock):
    return lax.dot_general(
        query, keyblock, (((1,), (1,)), ((), ())), preferred_element_type=jnp.float32
    )


def mix_block(weights, valueblock):
    return jnp.dot(weights, valueblock, preferred_element_type=jnp.float32)


def normalize(scores, visible, inv_scale):
    scores = jnp.where(visible, scores * inv_scale, -jnp.inf)
    top = jnp.max(scores, axis=-1, keepdims=True)
    expo = jnp.exp(scores - top)
    return (expo / jnp.sum(expo, axis=-1, keepdims=True)).astype(jnp.bfloat16)


def body(
    hidden,
    attention_norm_gain,
    wq,
    adapter_down_weight,
    adapter_up_weight,
    key_value_cache,
    logical_page_table,
    lengths,
    prompt_adapter_index,
):
    token_device_rows = hidden.shape[0]
    page_index = lax.axis_index("page")
    head_index = lax.axis_index("head")
    span_count = lax.axis_size("page") // 4
    x = hidden.astype(jnp.float32)
    scale_rows = lax.rsqrt(jnp.mean(x * x, axis=-1, keepdims=True) + EPSILON)
    normed_input = (x * scale_rows * attention_norm_gain.astype(jnp.float32)).astype(jnp.bfloat16)
    ends = jnp.cumsum(lengths)
    starts = ends - lengths
    token = page_index * token_device_rows + jnp.arange(token_device_rows, dtype=jnp.int32)
    member = (token[:, None] >= starts[None, :]) & (token[:, None] < ends[None, :])
    tok_start = jnp.sum(jnp.where(member, starts[None, :], 0), axis=1)
    tok_adapter = jnp.sum(jnp.where(member, prompt_adapter_index[None, :], 0), axis=1)
    token_position = token - tok_start
    q_cols = wq.shape[1]
    base_query = jnp.dot(
        normed_input,
        lax.all_gather(wq, "page", axis=0, tiled=True),
        preferred_element_type=jnp.float32,
    )
    shrink_all, expand_every_token = (
        lax.all_gather(adapter_down_weight, "page", axis=1, tiled=True),
        lax.all_gather(adapter_up_weight, "page", axis=0, tiled=True),
    )
    adapter_count = shrink_all.shape[1] // ADAPTER_RANK
    feature_number = adapter_down_weight.shape[0]
    own_features = lax.dynamic_slice_in_dim(
        normed_input, head_index * feature_number, feature_number, 1
    )
    partial_every_token = jnp.dot(own_features, shrink_all, preferred_element_type=jnp.float32)
    partial_every_token = partial_every_token.reshape(
        token_device_rows, adapter_count, ADAPTER_RANK
    )
    pick = tok_adapter[:, None] == jnp.arange(adapter_count, dtype=jnp.int32)[None, :]
    partial_sum = jnp.sum(jnp.where(pick[:, :, None], partial_every_token, 0.0), axis=1)
    shrunk = lax.psum(partial_sum, "head").astype(jnp.bfloat16)
    spread_heads = jnp.where(pick[:, :, None], shrunk[:, None, :], jnp.zeros((), jnp.bfloat16))
    spread_heads = spread_heads.reshape(token_device_rows, adapter_count * ADAPTER_RANK)
    adapter_delta = jnp.dot(spread_heads, expand_every_token, preferred_element_type=jnp.float32)
    local_head_count = q_cols // HEAD_WIDTH
    queries = apply_rotation(
        (base_query + adapter_delta).reshape(token_device_rows, local_head_count, HEAD_WIDTH),
        token_position,
        HEAD_WIDTH,
    ).astype(jnp.bfloat16)
    kv_width = key_value_cache.shape[2]
    kv_heads = kv_width // HEAD_WIDTH
    page_count = logical_page_table.shape[1]
    paged = key_value_cache.reshape(page_count, token_device_rows // page_count, 2, kv_width)
    own_block = jnp.take(paged, logical_page_table[0], axis=0).reshape(
        token_device_rows, 2, kv_width
    )

    def pass_on(moving, unused):
        moved = from_behind(moving, "page", 1)
        return (moved, moved)

    unused_last, earlier = lax.scan(pass_on, own_block, None, length=span_count)
    stacked = jnp.concatenate([earlier[::-1], own_block[None]], axis=0)
    block_count = span_count + 1
    key_total = block_count * token_device_rows
    key_index = (page_index - span_count) * token_device_rows + jnp.arange(
        key_total, dtype=jnp.int32
    )
    visible = (key_index[None, :] >= tok_start[:, None]) & (key_index[None, :] <= token[:, None])
    inv_scale = 1.0 / math.sqrt(HEAD_WIDTH)
    group = local_head_count // kv_heads
    outputs = []
    for kv_head in range(kv_heads):
        low = kv_head * HEAD_WIDTH
        key_stack = stacked[:, :, 0, low : low + HEAD_WIDTH]
        value_stack = stacked[:, :, 1, low : low + HEAD_WIDTH]
        for member_head in range(group):
            query = queries[:, kv_head * group + member_head]
            keys_joined = key_stack.reshape(key_total, HEAD_WIDTH)
            values_joined = value_stack.reshape(key_total, HEAD_WIDTH)
            weights = normalize(score_block(query, keys_joined), visible, inv_scale)
            outputs.append(mix_block(weights, values_joined))
    attended = jnp.stack(outputs, axis=1).reshape(token_device_rows, q_cols).astype(jnp.bfloat16)
    return (queries.reshape(token_device_rows, q_cols), attended)


PAIR = 4


def swap(value, bit):
    count = lax.axis_size("page")
    return lax.ppermute(value, "page", [(p, p ^ bit) for p in range(count)])


def shift_z(value, steps):
    count = lax.axis_size("page")
    return lax.ppermute(value, "page", [(p, (p + 8 * steps) % count) for p in range(count)])


class Transfers:
    def __init__(self):
        self.found = {}

    def __getitem__(self, name):
        return self.found[name]

    def tie(self, values, waits):
        waits = list(waits)
        tied = lax.optimization_barrier((*values, *[self.found[name] for name in waits]))
        for name, value in zip(waits, tied[len(values) :]):
            self.found[name] = value
        return list(tied[: len(values)])

    def run(self, waits, sends):
        operands = [operand for _, operand, _ in sends]
        if waits:
            operands = self.tie(operands, waits)
        for (name, _, move), operand in zip(sends, operands):
            self.found[name] = move(operand)


def in_order(flag, one, other):
    return jnp.where(
        flag == 0,
        jnp.concatenate([one, other], axis=0),
        jnp.concatenate([other, one], axis=0),
    )


def member_rows(value, first_token, starts, ends):
    token = first_token + lax.broadcasted_iota(jnp.int32, (1, value.shape[1]), 1)
    return [
        jnp.where((token >= start) & (token < end), value, 0.0) for start, end in zip(starts, ends)
    ]


def choose_kernel(which, every_ref, out_ref, held, sems):
    slots = which.shape[0]
    rank = every_ref.shape[1] // 2
    copies = []
    for r in range(slots):
        for kind in range(2):
            copies.append(
                pltpu.make_async_copy(
                    every_ref.at[which[r], pl.ds(kind * rank, rank)],
                    held.at[pl.ds((kind * slots + r) * rank, rank)],
                    sems.at[kind, r],
                )
            )
    for copy in copies:
        copy.start()
    for copy in copies:
        copy.wait()
    rows, width = out_ref.shape
    part = held.shape[1]
    for h in range(width // part):
        out_ref[:, h * part : (h + 1) * part] = held[h * rows : (h + 1) * rows]


def choose(which, every, width):
    slots = which.shape[0]
    _, rows, part = every.shape
    return pl.pallas_call(
        choose_kernel,
        out_shape=jax.ShapeDtypeStruct((slots * rows * part // width, width), every.dtype),
        in_specs=[pl.BlockSpec(memory_space=pltpu.SMEM), pl.BlockSpec(memory_space=pl.ANY)],
        out_specs=pl.BlockSpec(memory_space=pltpu.VMEM),
        scratch_shapes=[
            pltpu.VMEM((slots * rows, part), every.dtype),
            pltpu.SemaphoreType.DMA((2, slots)),
        ],
        cost_estimate=pl.CostEstimate(flops=1000, bytes_accessed=1000, transcendentals=0),
        name="choose",
    )(which, every)


def shrink_kernel(layout, blocks, part, numbers, *refs):
    normed_refs, refs = refs[: len(layout)], refs[len(layout) :]
    near_ref, far_ref, out_ref, up_ref, held, adapters, normed_sems, sems = refs
    rank, columns = out_ref.shape
    rows = columns // PAIR
    features = held.shape[2]
    slots = adapters.shape[0] // (2 * rank)
    extra = near_ref.shape[0] * 2 // blocks
    quarter = numbers[0]
    columns_here = pl.ds(pl.multiple_of(quarter * features, features), features)
    copies = [
        pltpu.make_async_copy(
            ref.at[:, columns_here], held.at[i, pl.ds(low, ref.shape[0])], normed_sems.at[n]
        )
        for n, (ref, (i, low)) in enumerate(zip(normed_refs, layout))
    ]
    for b in range(blocks):
        place = pl.multiple_of(numbers[1 + b] * part, part)
        source = (near_ref, far_ref)[b % 2].at[pl.ds(b // 2 * extra, extra)]
        for h in range(2 * slots * rank // extra):
            copies.append(
                pltpu.make_async_copy(
                    source.at[:, pl.ds(h * part, part)],
                    adapters.at[pl.ds(h * extra, extra), pl.ds(place, part)],
                    sems.at[b, h],
                )
            )
    for copy in copies:
        copy.start()
    for copy in copies:
        copy.wait()
    up_ref[...] = adapters[slots * rank :]
    at = 1 + blocks + PAIR
    starts = [numbers[at + r] for r in range(slots)]
    ends = [numbers[at + slots + r] for r in range(slots)]
    for i in range(PAIR):
        partial = lax.dot_general(
            adapters[: slots * rank],
            held[i],
            (((1,), (1,)), ((), ())),
            preferred_element_type=jnp.float32,
        )
        token = numbers[1 + blocks + i] + lax.broadcasted_iota(jnp.int32, (1, rows), 1)
        found = jnp.zeros((rank, rows), jnp.float32)
        for r in range(slots):
            member = (token >= starts[r]) & (token < ends[r])
            found += jnp.where(member, partial[r * rank : (r + 1) * rank], 0.0)
        place = pl.multiple_of((quarter ^ i) * rows, HEAD_WIDTH)
        out_ref[:, pl.ds(place, rows)] = found


def shrink(numbers, layout, normed, near, far, blocks, part, slots, rank):
    rows, _ = normed[0].shape
    extra, width = near.shape[0] * 2 // blocks, blocks * part
    vmem = pl.BlockSpec(memory_space=pltpu.VMEM)
    return pl.pallas_call(
        functools.partial(shrink_kernel, layout, blocks, part),
        out_shape=(
            jax.ShapeDtypeStruct((rank, PAIR * rows), jnp.float32),
            jax.ShapeDtypeStruct((slots * rank, width), jnp.bfloat16),
        ),
        in_specs=[pl.BlockSpec(memory_space=pltpu.SMEM)]
        + [pl.BlockSpec(memory_space=pl.ANY)] * (len(layout) + 2),
        out_specs=(vmem, vmem),
        scratch_shapes=[
            pltpu.VMEM((PAIR, rows, width), jnp.bfloat16),
            pltpu.VMEM((2 * slots * rank, width), jnp.bfloat16),
            pltpu.SemaphoreType.DMA((len(layout),)),
            pltpu.SemaphoreType.DMA((blocks, 2 * slots * rank // extra)),
        ],
        compiler_params=pltpu.CompilerParams(vmem_limit_bytes=60 * 1024 * 1024),
        cost_estimate=pl.CostEstimate(flops=1000, bytes_accessed=1000, transcendentals=0),
        name="shrink",
    )(numbers, *normed, near, far)


def project_kernel(layout, spots, numbers, *refs):
    blocks = len(spots)
    arrays = 1 + max(which for which, _ in spots)
    normed_refs, refs = refs[: len(layout)], refs[len(layout) :]
    weight_refs, refs = refs[:arrays], refs[arrays:]
    shrunk_ref, up_ref, cosine_ref, sine_ref, home_ref, away_ref, held, weight, sems = refs
    _, rows, width = home_ref.shape
    depth = weight.shape[0] // blocks
    rank = shrunk_ref.shape[0]
    slots = up_ref.shape[0] // rank
    weight_copies = [
        pltpu.make_async_copy(
            weight_refs[spots[b][0]].at[pl.ds(spots[b][1], depth)],
            weight.at[pl.ds(pl.multiple_of(numbers[1 + b] * depth, depth), depth)],
            sems.at[len(layout) + b],
        )
        for b in range(blocks)
    ]
    copies = [
        pltpu.make_async_copy(ref, held.at[i, pl.ds(low, ref.shape[0])], sems.at[n])
        for n, (ref, (i, low)) in enumerate(zip(normed_refs, layout))
    ]
    for copy in weight_copies + copies:
        copy.start()
    for copy in weight_copies:
        copy.wait()
    at = 1 + blocks + PAIR
    starts = [numbers[at + r] for r in range(slots)]
    ends = [numbers[at + slots + r] for r in range(slots)]
    for i in range(PAIR):
        for copy, (block, _) in zip(copies, layout):
            if block == i:
                copy.wait()
        block = numbers[0] ^ i
        place = pl.multiple_of(block * rows, HEAD_WIDTH)
        shrunk = shrunk_ref[:, pl.ds(place, rows)].astype(jnp.float32)
        spread = member_rows(shrunk, numbers[1 + blocks + i], starts, ends)
        spread = jnp.concatenate(spread, axis=0).astype(jnp.bfloat16)
        total = lax.dot_general(
            spread, up_ref[...], (((0,), (0,)), ((), ())), preferred_element_type=jnp.float32
        )
        total += jnp.dot(held[i], weight[...], preferred_element_type=jnp.float32)
        cosine = cosine_ref[block]
        sine = sine_ref[block]
        for low in range(0, width, HEAD_WIDTH):
            head = total[:, low : low + HEAD_WIDTH]
            turned = head * cosine + pltpu.roll(head, HEAD_WIDTH // 2, 1) * sine
            out_ref = (home_ref, away_ref)[i // 2]
            out_ref[i % 2, :, low : low + HEAD_WIDTH] = turned.astype(jnp.bfloat16)


def project(numbers, layout, spots, normed, weights, shrunk, up, cosine, sine):
    rows, features = normed[0].shape
    width = weights[0].shape[1]
    blocks = len(spots)
    vmem = pl.BlockSpec(memory_space=pltpu.VMEM)
    return pl.pallas_call(
        functools.partial(project_kernel, layout, spots),
        out_shape=(jax.ShapeDtypeStruct((PAIR // 2, rows, width), jnp.bfloat16),) * 2,
        in_specs=[pl.BlockSpec(memory_space=pltpu.SMEM)]
        + [pl.BlockSpec(memory_space=pl.ANY)] * (len(layout) + len(weights))
        + [vmem] * 4,
        out_specs=(vmem, vmem),
        scratch_shapes=[
            pltpu.VMEM((PAIR, rows, features), jnp.bfloat16),
            pltpu.VMEM((features, width), jnp.bfloat16),
            pltpu.SemaphoreType.DMA((len(layout) + blocks,)),
        ],
        compiler_params=pltpu.CompilerParams(vmem_limit_bytes=60 * 1024 * 1024),
        cost_estimate=pl.CostEstimate(flops=1000, bytes_accessed=1000, transcendentals=0),
        name="project",
    )(numbers, *normed, *weights, shrunk, up, cosine, sine)


def largest_square(value):
    wide = value.astype(jnp.float32)
    ones = jnp.ones((HEAD_WIDTH, HEAD_WIDTH), jnp.bfloat16)
    sums = jnp.dot((wide * wide).astype(jnp.bfloat16), ones, preferred_element_type=jnp.float32)
    return jnp.max(sums, axis=0, keepdims=True)


def window_kernel(
    column, numbers, older_ref, old_ref, own_ref, keys, turned, longest, values, sems
):
    rows = own_ref.shape[0] // PAIR
    value_column = own_ref.shape[1] // 2 + column
    copies = []
    for kind, (low, target) in enumerate(((value_column, values), (column, keys))):
        for b, source in enumerate((older_ref, old_ref, own_ref)):
            for i in range(PAIR):
                place = pl.multiple_of(numbers[i] + b * PAIR * rows, rows)
                copies.append(
                    pltpu.make_async_copy(
                        source.at[pl.ds(i * rows, rows), pl.ds(low, HEAD_WIDTH)],
                        target.at[pl.ds(place, rows)],
                        sems.at[kind, b * PAIR + i],
                    )
                )
    for copy in copies:
        copy.start()
    turned[HEAD_WIDTH:] = jnp.ones(
        (turned.shape[0] - HEAD_WIDTH, turned.shape[1]), jnp.bfloat16
    )
    longest[...] = jnp.zeros(longest.shape, jnp.float32)
    for copy in copies:
        copy.wait()

    def turn(i, carry):
        part = pl.ds(pl.multiple_of(i * KEY_TILE, KEY_TILE), KEY_TILE)
        turned[:HEAD_WIDTH, part] = values[part].T
        longest[...] = jnp.maximum(longest[...], largest_square(keys[part]))
        return carry

    lax.fori_loop(0, keys.shape[0] // KEY_TILE, turn, 0)


def window(column, numbers, older, old, own):
    key_total = 3 * own.shape[0]
    vmem = pl.BlockSpec(memory_space=pltpu.VMEM)
    return pl.pallas_call(
        functools.partial(window_kernel, column),
        out_shape=(
            jax.ShapeDtypeStruct((key_total, HEAD_WIDTH), jnp.bfloat16),
            jax.ShapeDtypeStruct((HEAD_WIDTH + 16, key_total), jnp.bfloat16),
            jax.ShapeDtypeStruct((1, HEAD_WIDTH), jnp.float32),
        ),
        in_specs=[pl.BlockSpec(memory_space=pltpu.SMEM)]
        + [pl.BlockSpec(memory_space=pl.ANY)] * 3,
        out_specs=(vmem, vmem, vmem),
        scratch_shapes=[
            pltpu.VMEM((key_total, HEAD_WIDTH), jnp.bfloat16),
            pltpu.SemaphoreType.DMA((2, 3 * PAIR)),
        ],
        compiler_params=pltpu.CompilerParams(vmem_limit_bytes=60 * 1024 * 1024),
        cost_estimate=pl.CostEstimate(flops=1000, bytes_accessed=1000, transcendentals=0),
        name="window",
    )(numbers, older, old, own)


def attend_kernel(
    numbers, start_ref, query_ref, keys, turned, longest, out_ref, total, top_ref
):
    step = pl.program_id(0)
    tiles = pl.num_programs(0)
    _, tile_rows, width = query_ref.shape
    group = width // HEAD_WIDTH
    first_token = numbers[step]
    low_start = numbers[tiles + step]
    base = numbers[2 * tiles]
    factor = math.log2(math.e) / math.sqrt(HEAD_WIDTH)
    queries = [query_ref[0, :, h * HEAD_WIDTH : (h + 1) * HEAD_WIDTH] for h in range(group)]
    bound = functools.reduce(jnp.maximum, [largest_square(part) for part in queries])
    small = jnp.max(bound * longest[...]) * (factor * factor) < SAFE_POWER * SAFE_POWER
    total[...] = jnp.zeros(total.shape, jnp.float32)
    top_ref[...] = jnp.full(top_ref.shape, LOWEST, jnp.float32)

    def add(tile, careful):
        low = pl.multiple_of(tile * KEY_TILE, KEY_TILE)
        here = keys[pl.ds(low, KEY_TILE)]
        shape = (KEY_TILE, tile_rows)
        key_index = base + low + lax.broadcasted_iota(jnp.int32, shape, 0)
        token = first_token + lax.broadcasted_iota(jnp.int32, shape, 1)
        seen = (key_index <= token) & (key_index >= start_ref[0])
        products = [
            lax.dot_general(
                here, query, (((1,), (1,)), ((), ())), preferred_element_type=jnp.float32
            )
            for query in queries
        ]
        for h in range(group):
            power = jnp.where(seen, products[h] * factor, LOWEST)
            before = total[h]
            if careful:
                old_top = top_ref[h]
                new_top = jnp.maximum(old_top, jnp.max(power, axis=0, keepdims=True))
                top_ref[h] = new_top
                power = power - new_top
                before = before * jnp.exp2(old_top - new_top)
            total[h] = before + jnp.dot(
                turned[:, pl.ds(low, KEY_TILE)],
                jnp.exp2(power).astype(jnp.bfloat16),
                preferred_element_type=jnp.float32,
            )

    def plain_tile(tile, carry):
        add(tile, False)
        return carry

    def careful_tile(tile, carry):
        add(tile, True)
        return carry

    from_tile = (low_start - base) // KEY_TILE
    to_tile = (first_token + tile_rows - 1 - base) // KEY_TILE + 1
    middle = jnp.where(small, to_tile, from_tile)
    lax.fori_loop(from_tile, middle, plain_tile, 0)
    lax.fori_loop(middle, to_tile, careful_tile, 0)
    for h in range(group):
        mixed = total[h, :HEAD_WIDTH] / total[h, HEAD_WIDTH : HEAD_WIDTH + 1]
        out_ref[0, :, h * HEAD_WIDTH : (h + 1) * HEAD_WIDTH] = mixed.T.astype(jnp.bfloat16)


def attend(numbers, tile_starts, queries, keys, turned, longest):
    tiles, tile_rows, width = queries.shape
    group = width // HEAD_WIDTH
    deep = turned.shape[0]

    def whole(array):
        return pl.BlockSpec(array.shape, lambda i, n: (0, 0))

    return pl.pallas_call(
        attend_kernel,
        grid_spec=pltpu.PrefetchScalarGridSpec(
            num_scalar_prefetch=1,
            grid=(tiles,),
            in_specs=[
                pl.BlockSpec((1, 1, tile_rows), lambda i, n: (i, 0, 0)),
                pl.BlockSpec((1, tile_rows, width), lambda i, n: (i, 0, 0)),
                whole(keys),
                whole(turned),
                whole(longest),
            ],
            out_specs=pl.BlockSpec((1, tile_rows, width), lambda i, n: (i, 0, 0)),
            scratch_shapes=[
                pltpu.VMEM((group, deep, tile_rows), jnp.float32),
                pltpu.VMEM((group, 1, tile_rows), jnp.float32),
            ],
        ),
        out_shape=jax.ShapeDtypeStruct(queries.shape, jnp.bfloat16),
        compiler_params=pltpu.CompilerParams(vmem_limit_bytes=60 * 1024 * 1024),
        cost_estimate=pl.CostEstimate(flops=1000, bytes_accessed=1000, transcendentals=0),
        name="attend",
    )(numbers, tile_starts, queries, keys, turned, longest)


def place_kernel(numbers, *refs):
    sources, outs, (held, sems, out_sems) = refs[:-5], refs[-5:-3], refs[-3:]
    width = sources[0].shape[2]
    each = len(sources) // len(outs)
    copies = [
        pltpu.make_async_copy(
            source.at[numbers[2 * n]],
            held.at[n // each, :, pl.ds(pl.multiple_of(numbers[2 * n + 1], width), width)],
            sems.at[n],
        )
        for n, source in enumerate(sources)
    ]
    for copy in copies:
        copy.start()
    last = [
        pltpu.make_async_copy(held.at[kind], out, out_sems.at[kind])
        for kind, out in enumerate(outs)
    ]
    for kind, whole in enumerate(last):
        for copy in copies[kind * each : (kind + 1) * each]:
            copy.wait()
        whole.start()
    for whole in last:
        whole.wait()


def place(blocks, columns):
    numbers = jnp.stack([n for _, index, low in blocks for n in (index, low)]).astype(jnp.int32)
    arrays = [array for array, _, _ in blocks]
    _, rows, _ = arrays[0].shape
    return pl.pallas_call(
        place_kernel,
        out_shape=(jax.ShapeDtypeStruct((rows, columns), arrays[0].dtype),) * 2,
        in_specs=[pl.BlockSpec(memory_space=pltpu.SMEM)]
        + [pl.BlockSpec(memory_space=pl.ANY)] * len(blocks),
        out_specs=(pl.BlockSpec(memory_space=pl.ANY),) * 2,
        scratch_shapes=[
            pltpu.VMEM((2, rows, columns), arrays[0].dtype),
            pltpu.SemaphoreType.DMA((len(blocks),)),
            pltpu.SemaphoreType.DMA((2,)),
        ],
        compiler_params=pltpu.CompilerParams(vmem_limit_bytes=60 * 1024 * 1024),
        cost_estimate=pl.CostEstimate(flops=1000, bytes_accessed=1000, transcendentals=0),
        name="place",
    )(numbers, *arrays)


def pair_body(
    hidden,
    attention_norm_gain,
    wq,
    adapter_down_weight,
    adapter_up_weight,
    key_value_cache,
    logical_page_table,
    lengths,
    prompt_adapter_index,
):
    rows, features = hidden.shape
    count = lax.axis_size("page")
    me = lax.axis_index("page")
    core, x, y, z = me % 2, (me // 2) % 2, (me // 4) % 2, me // 8
    pair = me // PAIR
    quarter = me % PAIR
    q_cols = wq.shape[1]
    width = q_cols // PAIR
    kv_width = key_value_cache.shape[2]
    kv_part = kv_width // PAIR
    kv_heads = kv_part // HEAD_WIDTH
    chunk = width // kv_heads

    def weight_part(part_x, part_core):
        return lax.dynamic_slice_in_dim(wq, (2 * part_x + part_core) * width, width, 1)

    sent = Transfers()
    core_swap = functools.partial(swap, bit=1)
    x_swap = functools.partial(swap, bit=2)
    y_swap = functools.partial(swap, bit=4)
    wq_rows = wq.shape[0]
    wq_depth = PAIR * wq_rows
    pairs = count // PAIR
    z_count = count // 8
    order = (0, 1, 3, 2)

    rank = adapter_up_weight.shape[0]
    slots = prompt_adapter_index.shape[0]
    part = width // pairs
    both = jnp.concatenate([adapter_down_weight.T, adapter_up_weight], axis=0)
    both = both.reshape(2 * rank, PAIR, pairs, part).transpose(2, 1, 0, 3)
    both = both.reshape(count * 2 * rank, part)

    def exchange(value):
        return lax.all_to_all(value, "page", split_axis=0, concat_axis=0, tiled=True)

    sent.run([], [("adapters", both, exchange)])
    sent.run(
        [],
        [
            (
                "weight c",
                jnp.concatenate([weight_part(x, 1 - core), weight_part(1 - x, 1 - core)], axis=0),
                core_swap,
            )
        ],
    )
    from_core = sent["weight c"]
    mine = in_order(core, weight_part(1 - x, core), from_core[wq_rows:])
    kept = in_order(core, weight_part(x, core), from_core[:wq_rows])
    first_mine, key_value_cache = lax.optimization_barrier((mine[:, :chunk], key_value_cache))
    sent.run([], [("weight x0", first_mine, x_swap)])
    (hidden,) = sent.tie([hidden], ["weight x0"])

    page_count = logical_page_table.shape[1]
    page_rows = rows // page_count
    paged = key_value_cache.reshape(page_count, page_rows, 2, kv_width)
    ordered = jnp.concatenate(
        [
            lax.dynamic_index_in_dim(paged, logical_page_table[0, j], 0, keepdims=False)
            for j in range(page_count)
        ],
        axis=0,
    ).reshape(rows, 2 * kv_width)

    def cache_part(part_x, part_core):
        low = (2 * part_x + part_core) * kv_part
        return jnp.concatenate(
            [
                lax.dynamic_slice_in_dim(ordered, low, kv_part, 1),
                lax.dynamic_slice_in_dim(ordered, kv_width + low, kv_part, 1),
            ],
            axis=1,
        )

    sent.run(
        [],
        [
            (
                "cache c",
                jnp.concatenate([cache_part(x, 1 - core), cache_part(1 - x, 1 - core)], axis=0),
                core_swap,
            )
        ],
    )
    cache_core = sent["cache c"]

    wide = hidden.astype(jnp.float32)
    scale_rows = lax.rsqrt(jnp.mean(wide * wide, axis=-1, keepdims=True) + EPSILON)
    normed_own = (wide * scale_rows * attention_norm_gain.astype(jnp.float32)).astype(jnp.bfloat16)
    half_rows = rows // 2
    ends = jnp.cumsum(lengths)
    starts = ends - lengths
    first_token = pair * (PAIR * rows)
    token = first_token + jnp.arange(PAIR * rows, dtype=jnp.int32)
    member = (token[None, :] >= starts[:, None]) & (token[None, :] < ends[:, None])
    tok_start = jnp.sum(jnp.where(member, starts[:, None], 0), axis=0)
    position = (token - tok_start).astype(jnp.float32)
    half = HEAD_WIDTH // 2
    inverse = ROPE_BASE ** (-(jnp.arange(half, dtype=jnp.float32) * 2.0 / HEAD_WIDTH))
    angle = position[:, None] * inverse[None, :]
    cosine, sine = jnp.cos(angle), jnp.sin(angle)
    cosine = jnp.concatenate([cosine, cosine], axis=1).reshape(PAIR, rows, HEAD_WIDTH)
    sine = jnp.concatenate([-sine, sine], axis=1).reshape(PAIR, rows, HEAD_WIDTH)

    chosen = choose(prompt_adapter_index, sent["adapters"].reshape(count, 2 * rank, part), chunk)
    pieces = [in_order(x, kept[:, :chunk], sent["weight x0"])]

    def along_z(g, k):
        return (f"z{g} {k}", pieces[g], functools.partial(shift_z, steps=k))

    def along_y(g, k):
        return (f"y{g} {k}", sent[f"z{g} {k}"] if k else pieces[g], y_swap)

    def older(value):
        return lax.ppermute(value, "page", [(p, p + 8) for p in range(count - 8)])

    cuts = (0, rows // 2, rows)

    def normed_part(n):
        return (f"normed x{n}", normed_own[cuts[n] : cuts[n + 1]], x_swap)

    def normed_on(n):
        return (f"normed xc{n}", sent[f"normed x{n}"], core_swap)

    sent.run(
        ["weight x0"],
        [
            along_z(0, 1),
            along_z(0, 3),
            along_y(0, 0),
            ("weight x1", mine[:, chunk:], x_swap),
        ],
    )
    sent.run(
        [],
        [
            ("normed c", normed_own, core_swap),
            (
                "cache x",
                jnp.concatenate([cache_part(1 - x, core), cache_core[rows:]], axis=0),
                x_swap,
            ),
        ],
    )
    pieces.append(in_order(x, kept[:, chunk:], sent["weight x1"]))
    sent.run(
        ["z0 1", "z0 3", "y0 0", "weight x1", "cache x", "normed c"],
        [
            along_z(0, 2),
            along_z(1, 1),
            ("y0 1 3", jnp.concatenate([sent["z0 1"], sent["z0 3"]], axis=0), y_swap),
            along_y(1, 0),
            normed_part(0),
        ]
        + [
            (f"adapters z{k}", chosen, functools.partial(shift_z, steps=k)) for k in order[1:]
        ],
    )
    cache_own = jnp.concatenate([cache_part(x, core), cache_core[:rows], sent["cache x"]], axis=0)
    cosine, sine = sent.tie([cosine, sine], ["y1 0"])
    sent.run(
        ["z0 2", "z1 1", "y0 1 3", "y1 0", "normed x0"]
        + [f"adapters z{k}" for k in order[1:]],
        [
            ("cache z", cache_own, older),
            along_y(0, 2),
            along_y(1, 1),
            normed_part(1),
            normed_on(0),
            (
                "adapters y",
                jnp.concatenate(
                    [chosen] + [sent[f"adapters z{k}"] for k in order[1:]], axis=0
                ),
                y_swap,
            ),
        ],
    )
    adapters_near = jnp.concatenate(
        [chosen] + [sent[f"adapters z{k}"] for k in order[1:]], axis=0
    )
    sent.run(
        ["cache z", "y0 2", "y1 1", "normed x1", "normed xc0", "adapters y"],
        [
            normed_on(1),
            along_z(1, 3),
            along_z(1, 2),
            ("cache y", jnp.where(y == 1, sent["cache z"], cache_own), y_swap),
        ],
    )
    normed = [normed_own, sent["normed c"]]
    normed += [sent[f"normed {way}{n}"] for way in ("x", "xc") for n in range(2)]
    layout = ((0, 0), (1, 0)) + tuple((i, cuts[n]) for i in (2, 3) for n in range(2))

    members = jnp.arange(PAIR, dtype=jnp.int32)
    places = [((z - k) % z_count) * 2 + (y ^ dy) for k in order for dy in (0, 1)]
    numbers = jnp.concatenate(
        [
            quarter[None],
            jnp.stack(places),
            first_token + (quarter ^ members) * rows,
            starts,
            ends,
        ]
    ).astype(jnp.int32)
    partial, up = shrink(
        numbers,
        layout,
        normed,
        adapters_near,
        sent["adapters y"],
        2 * z_count,
        part,
        slots,
        rank,
    )
    partial = partial + swap(partial, 1)
    partial = partial + swap(partial, 2)
    shrunk = partial.astype(jnp.bfloat16)

    def project_part(g, spots, weights, shrunk):
        return project(
            numbers, layout, spots, normed, weights, shrunk, up[:, g * chunk : (g + 1) * chunk], cosine, sine
        )

    block_starts = jnp.stack(
        [lax.dynamic_slice_in_dim(tok_start, (quarter ^ i) * rows, rows, 0) for i in range(PAIR)]
    ).reshape(PAIR, 1, rows)

    def attend_part(g, first, queries):
        tiles = queries.shape[0]
        here = block_starts[first : first + tiles]
        steps = jnp.concatenate(
            [
                first_token + (quarter ^ members[first : first + tiles]) * rows,
                here[:, 0, 0],
                (first_token - 2 * PAIR * rows)[None],
            ]
        ).astype(jnp.int32)
        return attend(steps, here, queries, *windows[g])

    def home(name, g, value):
        from_x = sent[f"{name} x{g}"]
        from_core = swap(jnp.stack([value[1], from_x[1]]), 1)
        found = ((0, value, 0), (2, from_x, 0), (1, from_core, 0), (3, from_core, 1))
        return [
            (array, jnp.int32(which), (quarter ^ bits) * width + g * chunk)
            for bits, array, which in found
        ]

    depth = wq_depth
    home0, away0 = project_part(
        0,
        ((0, 0), (1, 0), (2, 0), (5, 0), (3, 0), (5, depth), (4, 0), (6, 0)),
        [pieces[0]]
        + [sent[name] for name in ("y0 0", "z0 1", "z0 3", "z0 2", "y0 1 3", "y0 2")],
        shrunk,
    )
    away0, home0, cache_old = lax.optimization_barrier((away0, home0, sent["cache y"]))
    windows = [
        window(
            g * HEAD_WIDTH,
            ((quarter ^ members) * rows).astype(jnp.int32),
            sent["cache z"],
            cache_old,
            cache_own,
        )
        for g in range(kv_heads)
    ]

    sent.run([], [("queries x0", away0, x_swap)])
    attended_away0 = attend_part(0, 2, away0)
    attended_away0, last3, last2 = lax.optimization_barrier(
        (attended_away0, sent["z1 3"], sent["z1 2"])
    )
    sent.run(
        ["cache y"],
        [
            ("y1 3 2", jnp.concatenate([last3, last2], axis=0), y_swap),
            ("attended x0", attended_away0, x_swap),
        ],
    )
    attended_home0 = attend_part(0, 0, home0)
    shrunk, attended_home0, *windows[1] = lax.optimization_barrier(
        (shrunk, attended_home0, *windows[1])
    )
    (shrunk,) = sent.tie([shrunk], ["queries x0"])
    home1, away1 = project_part(
        1,
        ((0, 0), (1, 0), (2, 0), (5, 0), (3, 0), (6, 0), (4, 0), (6, depth)),
        [pieces[1]]
        + [sent[name] for name in ("y1 0", "z1 1", "z1 3", "z1 2", "y1 1", "y1 3 2")],
        shrunk,
    )
    sent.run([], [("queries x1", away1, x_swap)])
    (away1,) = sent.tie([away1], ["attended x0"])
    attended_away1 = attend_part(1, 2, away1)
    sent.run(["queries x1"], [("attended x1", attended_away1, x_swap)])
    attended_home1 = attend_part(1, 0, home1)
    return tuple(
        place(
            home("queries", 0, home0)
            + home("queries", 1, home1)
            + home("attended", 0, attended_home0)
            + home("attended", 1, attended_home1),
            q_cols,
        )
    )


def solution(mesh):
    page, head = mesh.shape["page"], mesh.shape["head"]
    return jax.shard_map(
        pair_body if head == 1 and page == 32 else body,
        mesh=mesh,
        in_specs=(
            P("page", None),
            P(),
            P("page", "head"),
            P("head", "page"),
            P("page", "head"),
            P("page", None, "head"),
            P("page", None),
            P(),
            P(),
        ),
        out_specs=(P("page", "head"), P("page", "head")),
        check_vma=False,
    )
```

```python
import functools
import math

import jax
import jax.numpy as jnp
from jax import lax
from jax.experimental import pallas as pl
from jax.experimental.pallas import tpu as pltpu
from jax.sharding import PartitionSpec as P

HEAD_WIDTH = 128
ADAPTER_RANK = 16


EPSILON = 1e-05
ROPE_BASE = 500000.0
KEY_TILE = 512
LOWEST = -1e30
SAFE_POWER = 90.0


def from_behind(value, axis, steps):
    count = lax.axis_size(axis)
    leading, last = (max(0, -steps), min(count, count - steps))
    return lax.ppermute(value, axis, [(source, source + steps) for source in range(leading, last)])


def apply_rotation(values_f, token_position, head_size):
    half = head_size // 2
    inverse = ROPE_BASE ** (-(jnp.arange(half, dtype=jnp.float32) * 2.0 / head_size))
    angle = token_position.astype(jnp.float32)[:, None] * inverse[None, :]
    cosine = jnp.cos(angle)[:, None, :]
    sine = jnp.sin(angle)[:, None, :]
    first = values_f[..., :half]
    second = values_f[..., half:]
    return jnp.concatenate(
        [first * cosine - second * sine, second * cosine + first * sine], axis=-1
    )


def score_block(query, keyblock):
    return lax.dot_general(
        query, keyblock, (((1,), (1,)), ((), ())), preferred_element_type=jnp.float32
    )


def mix_block(weights, valueblock):
    return jnp.dot(weights, valueblock, preferred_element_type=jnp.float32)


def normalize(scores, visible, inv_scale):
    scores = jnp.where(visible, scores * inv_scale, -jnp.inf)
    top = jnp.max(scores, axis=-1, keepdims=True)
    expo = jnp.exp(scores - top)
    return (expo / jnp.sum(expo, axis=-1, keepdims=True)).astype(jnp.bfloat16)


def body(
    hidden,
    attention_norm_gain,
    wq,
    adapter_down_weight,
    adapter_up_weight,
    key_value_cache,
    logical_page_table,
    lengths,
    prompt_adapter_index,
):
    token_device_rows = hidden.shape[0]
    page_index = lax.axis_index("page")
    head_index = lax.axis_index("head")
    span_count = lax.axis_size("page") // 4
    x = hidden.astype(jnp.float32)
    scale_rows = lax.rsqrt(jnp.mean(x * x, axis=-1, keepdims=True) + EPSILON)
    normed_input = (x * scale_rows * attention_norm_gain.astype(jnp.float32)).astype(jnp.bfloat16)
    ends = jnp.cumsum(lengths)
    starts = ends - lengths
    token = page_index * token_device_rows + jnp.arange(token_device_rows, dtype=jnp.int32)
    member = (token[:, None] >= starts[None, :]) & (token[:, None] < ends[None, :])
    tok_start = jnp.sum(jnp.where(member, starts[None, :], 0), axis=1)
    tok_adapter = jnp.sum(jnp.where(member, prompt_adapter_index[None, :], 0), axis=1)
    token_position = token - tok_start
    q_cols = wq.shape[1]
    base_query = jnp.dot(
        normed_input,
        lax.all_gather(wq, "page", axis=0, tiled=True),
        preferred_element_type=jnp.float32,
    )
    shrink_all, expand_every_token = (
        lax.all_gather(adapter_down_weight, "page", axis=1, tiled=True),
        lax.all_gather(adapter_up_weight, "page", axis=0, tiled=True),
    )
    adapter_count = shrink_all.shape[1] // ADAPTER_RANK
    feature_number = adapter_down_weight.shape[0]
    own_features = lax.dynamic_slice_in_dim(
        normed_input, head_index * feature_number, feature_number, 1
    )
    partial_every_token = jnp.dot(own_features, shrink_all, preferred_element_type=jnp.float32)
    partial_every_token = partial_every_token.reshape(
        token_device_rows, adapter_count, ADAPTER_RANK
    )
    pick = tok_adapter[:, None] == jnp.arange(adapter_count, dtype=jnp.int32)[None, :]
    partial_sum = jnp.sum(jnp.where(pick[:, :, None], partial_every_token, 0.0), axis=1)
    shrunk = lax.psum(partial_sum, "head").astype(jnp.bfloat16)
    spread_heads = jnp.where(pick[:, :, None], shrunk[:, None, :], jnp.zeros((), jnp.bfloat16))
    spread_heads = spread_heads.reshape(token_device_rows, adapter_count * ADAPTER_RANK)
    adapter_delta = jnp.dot(spread_heads, expand_every_token, preferred_element_type=jnp.float32)
    local_head_count = q_cols // HEAD_WIDTH
    queries = apply_rotation(
        (base_query + adapter_delta).reshape(token_device_rows, local_head_count, HEAD_WIDTH),
        token_position,
        HEAD_WIDTH,
    ).astype(jnp.bfloat16)
    kv_width = key_value_cache.shape[2]
    kv_heads = kv_width // HEAD_WIDTH
    page_count = logical_page_table.shape[1]
    paged = key_value_cache.reshape(page_count, token_device_rows // page_count, 2, kv_width)
    own_block = jnp.take(paged, logical_page_table[0], axis=0).reshape(
        token_device_rows, 2, kv_width
    )

    def pass_on(moving, unused):
        moved = from_behind(moving, "page", 1)
        return (moved, moved)

    unused_last, earlier = lax.scan(pass_on, own_block, None, length=span_count)
    stacked = jnp.concatenate([earlier[::-1], own_block[None]], axis=0)
    block_count = span_count + 1
    key_total = block_count * token_device_rows
    key_index = (page_index - span_count) * token_device_rows + jnp.arange(
        key_total, dtype=jnp.int32
    )
    visible = (key_index[None, :] >= tok_start[:, None]) & (key_index[None, :] <= token[:, None])
    inv_scale = 1.0 / math.sqrt(HEAD_WIDTH)
    group = local_head_count // kv_heads
    outputs = []
    for kv_head in range(kv_heads):
        low = kv_head * HEAD_WIDTH
        key_stack = stacked[:, :, 0, low : low + HEAD_WIDTH]
        value_stack = stacked[:, :, 1, low : low + HEAD_WIDTH]
        for member_head in range(group):
            query = queries[:, kv_head * group + member_head]
            keys_joined = key_stack.reshape(key_total, HEAD_WIDTH)
            values_joined = value_stack.reshape(key_total, HEAD_WIDTH)
            weights = normalize(score_block(query, keys_joined), visible, inv_scale)
            outputs.append(mix_block(weights, values_joined))
    attended = jnp.stack(outputs, axis=1).reshape(token_device_rows, q_cols).astype(jnp.bfloat16)
    return (queries.reshape(token_device_rows, q_cols), attended)


PAIR = 4


def swap(value, bit):
    count = lax.axis_size("page")
    return lax.ppermute(value, "page", [(p, p ^ bit) for p in range(count)])


def shift_z(value, steps):
    count = lax.axis_size("page")
    return lax.ppermute(value, "page", [(p, (p + 8 * steps) % count) for p in range(count)])


class Transfers:
    def __init__(self):
        self.found = {}

    def __getitem__(self, name):
        return self.found[name]

    def tie(self, values, waits):
        waits = list(waits)
        tied = lax.optimization_barrier((*values, *[self.found[name] for name in waits]))
        for name, value in zip(waits, tied[len(values) :]):
            self.found[name] = value
        return list(tied[: len(values)])

    def run(self, waits, sends):
        operands = [operand for _, operand, _ in sends]
        if waits:
            operands = self.tie(operands, waits)
        for (name, _, move), operand in zip(sends, operands):
            self.found[name] = move(operand)


def in_order(flag, one, other):
    return jnp.where(
        flag == 0,
        jnp.concatenate([one, other], axis=0),
        jnp.concatenate([other, one], axis=0),
    )


def member_rows(value, first_token, starts, ends):
    token = first_token + lax.broadcasted_iota(jnp.int32, (1, value.shape[1]), 1)
    return [
        jnp.where((token >= start) & (token < end), value, 0.0) for start, end in zip(starts, ends)
    ]


def choose_kernel(which, every_ref, out_ref, held, sems):
    slots = which.shape[0]
    rank = every_ref.shape[1] // 2
    copies = []
    for r in range(slots):
        for kind in range(2):
            copies.append(
                pltpu.make_async_copy(
                    every_ref.at[which[r], pl.ds(kind * rank, rank)],
                    held.at[pl.ds((kind * slots + r) * rank, rank)],
                    sems.at[kind, r],
                )
            )
    for copy in copies:
        copy.start()
    for copy in copies:
        copy.wait()
    rows, width = out_ref.shape
    part = held.shape[1]
    for h in range(width // part):
        out_ref[:, h * part : (h + 1) * part] = held[h * rows : (h + 1) * rows]


def choose(which, every, width):
    slots = which.shape[0]
    _, rows, part = every.shape
    return pl.pallas_call(
        choose_kernel,
        out_shape=jax.ShapeDtypeStruct((slots * rows * part // width, width), every.dtype),
        in_specs=[pl.BlockSpec(memory_space=pltpu.SMEM), pl.BlockSpec(memory_space=pl.ANY)],
        out_specs=pl.BlockSpec(memory_space=pltpu.VMEM),
        scratch_shapes=[
            pltpu.VMEM((slots * rows, part), every.dtype),
            pltpu.SemaphoreType.DMA((2, slots)),
        ],
        cost_estimate=pl.CostEstimate(flops=1000, bytes_accessed=1000, transcendentals=0),
        name="choose",
    )(which, every)


def shrink_kernel(layout, blocks, part, numbers, *refs):
    normed_refs, refs = refs[: len(layout)], refs[len(layout) :]
    near_ref, far_ref, out_ref, up_ref, held, adapters, normed_sems, sems = refs
    rank, columns = out_ref.shape
    rows = columns // PAIR
    features = held.shape[2]
    slots = adapters.shape[0] // (2 * rank)
    extra = near_ref.shape[0] * 2 // blocks
    quarter = numbers[0]
    columns_here = pl.ds(pl.multiple_of(quarter * features, features), features)
    copies = [
        pltpu.make_async_copy(
            ref.at[:, columns_here], held.at[i, pl.ds(low, ref.shape[0])], normed_sems.at[n]
        )
        for n, (ref, (i, low)) in enumerate(zip(normed_refs, layout))
    ]
    for b in range(blocks):
        place = pl.multiple_of(numbers[1 + b] * part, part)
        source = (near_ref, far_ref)[b % 2].at[pl.ds(b // 2 * extra, extra)]
        for h in range(2 * slots * rank // extra):
            copies.append(
                pltpu.make_async_copy(
                    source.at[:, pl.ds(h * part, part)],
                    adapters.at[pl.ds(h * extra, extra), pl.ds(place, part)],
                    sems.at[b, h],
                )
            )
    for copy in copies:
        copy.start()
    for copy in copies:
        copy.wait()
    up_ref[...] = adapters[slots * rank :]
    at = 1 + blocks + PAIR
    starts = [numbers[at + r] for r in range(slots)]
    ends = [numbers[at + slots + r] for r in range(slots)]
    for i in range(PAIR):
        partial = lax.dot_general(
            adapters[: slots * rank],
            held[i],
            (((1,), (1,)), ((), ())),
            preferred_element_type=jnp.float32,
        )
        token = numbers[1 + blocks + i] + lax.broadcasted_iota(jnp.int32, (1, rows), 1)
        found = jnp.zeros((rank, rows), jnp.float32)
        for r in range(slots):
            member = (token >= starts[r]) & (token < ends[r])
            found += jnp.where(member, partial[r * rank : (r + 1) * rank], 0.0)
        place = pl.multiple_of((quarter ^ i) * rows, HEAD_WIDTH)
        out_ref[:, pl.ds(place, rows)] = found


def shrink(numbers, layout, normed, near, far, blocks, part, slots, rank):
    rows, _ = normed[0].shape
    extra, width = near.shape[0] * 2 // blocks, blocks * part
    vmem = pl.BlockSpec(memory_space=pltpu.VMEM)
    return pl.pallas_call(
        functools.partial(shrink_kernel, layout, blocks, part),
        out_shape=(
            jax.ShapeDtypeStruct((rank, PAIR * rows), jnp.float32),
            jax.ShapeDtypeStruct((slots * rank, width), jnp.bfloat16),
        ),
        in_specs=[pl.BlockSpec(memory_space=pltpu.SMEM)]
        + [pl.BlockSpec(memory_space=pl.ANY)] * (len(layout) + 2),
        out_specs=(vmem, vmem),
        scratch_shapes=[
            pltpu.VMEM((PAIR, rows, width), jnp.bfloat16),
            pltpu.VMEM((2 * slots * rank, width), jnp.bfloat16),
            pltpu.SemaphoreType.DMA((len(layout),)),
            pltpu.SemaphoreType.DMA((blocks, 2 * slots * rank // extra)),
        ],
        compiler_params=pltpu.CompilerParams(vmem_limit_bytes=60 * 1024 * 1024),
        cost_estimate=pl.CostEstimate(flops=1000, bytes_accessed=1000, transcendentals=0),
        name="shrink",
    )(numbers, *normed, near, far)


def project_kernel(layout, spots, numbers, *refs):
    blocks = len(spots)
    arrays = 1 + max(which for which, _ in spots)
    normed_refs, refs = refs[: len(layout)], refs[len(layout) :]
    weight_refs, refs = refs[:arrays], refs[arrays:]
    shrunk_ref, up_ref, cosine_ref, sine_ref, home_ref, away_ref, held, weight, sems = refs
    _, rows, width = home_ref.shape
    depth = weight.shape[0] // blocks
    rank = shrunk_ref.shape[0]
    slots = up_ref.shape[0] // rank
    weight_copies = [
        pltpu.make_async_copy(
            weight_refs[spots[b][0]].at[pl.ds(spots[b][1], depth)],
            weight.at[pl.ds(pl.multiple_of(numbers[1 + b] * depth, depth), depth)],
            sems.at[len(layout) + b],
        )
        for b in range(blocks)
    ]
    copies = [
        pltpu.make_async_copy(ref, held.at[i, pl.ds(low, ref.shape[0])], sems.at[n])
        for n, (ref, (i, low)) in enumerate(zip(normed_refs, layout))
    ]
    for copy in weight_copies + copies:
        copy.start()
    for copy in weight_copies:
        copy.wait()
    at = 1 + blocks + PAIR
    starts = [numbers[at + r] for r in range(slots)]
    ends = [numbers[at + slots + r] for r in range(slots)]
    for i in range(PAIR):
        for copy, (block, _) in zip(copies, layout):
            if block == i:
                copy.wait()
        block = numbers[0] ^ i
        place = pl.multiple_of(block * rows, HEAD_WIDTH)
        shrunk = shrunk_ref[:, pl.ds(place, rows)].astype(jnp.float32)
        spread = member_rows(shrunk, numbers[1 + blocks + i], starts, ends)
        spread = jnp.concatenate(spread, axis=0).astype(jnp.bfloat16)
        total = lax.dot_general(
            spread, up_ref[...], (((0,), (0,)), ((), ())), preferred_element_type=jnp.float32
        )
        total += jnp.dot(held[i], weight[...], preferred_element_type=jnp.float32)
        cosine = cosine_ref[block]
        sine = sine_ref[block]
        for low in range(0, width, HEAD_WIDTH):
            head = total[:, low : low + HEAD_WIDTH]
            turned = head * cosine + pltpu.roll(head, HEAD_WIDTH // 2, 1) * sine
            out_ref = (home_ref, away_ref)[i // 2]
            out_ref[i % 2, :, low : low + HEAD_WIDTH] = turned.astype(jnp.bfloat16)


def project(numbers, layout, spots, normed, weights, shrunk, up, cosine, sine):
    rows, features = normed[0].shape
    width = weights[0].shape[1]
    blocks = len(spots)
    vmem = pl.BlockSpec(memory_space=pltpu.VMEM)
    return pl.pallas_call(
        functools.partial(project_kernel, layout, spots),
        out_shape=(jax.ShapeDtypeStruct((PAIR // 2, rows, width), jnp.bfloat16),) * 2,
        in_specs=[pl.BlockSpec(memory_space=pltpu.SMEM)]
        + [pl.BlockSpec(memory_space=pl.ANY)] * (len(layout) + len(weights))
        + [vmem] * 4,
        out_specs=(vmem, vmem),
        scratch_shapes=[
            pltpu.VMEM((PAIR, rows, features), jnp.bfloat16),
            pltpu.VMEM((features, width), jnp.bfloat16),
            pltpu.SemaphoreType.DMA((len(layout) + blocks,)),
        ],
        compiler_params=pltpu.CompilerParams(vmem_limit_bytes=60 * 1024 * 1024),
        cost_estimate=pl.CostEstimate(flops=1000, bytes_accessed=1000, transcendentals=0),
        name="project",
    )(numbers, *normed, *weights, shrunk, up, cosine, sine)


def largest_square(value):
    wide = value.astype(jnp.float32)
    ones = jnp.ones((HEAD_WIDTH, HEAD_WIDTH), jnp.bfloat16)
    sums = jnp.dot((wide * wide).astype(jnp.bfloat16), ones, preferred_element_type=jnp.float32)
    return jnp.max(sums, axis=0, keepdims=True)


def window_kernel(
    column, numbers, older_ref, old_ref, own_ref, keys, turned, longest, values, sems
):
    rows = own_ref.shape[0] // PAIR
    value_column = own_ref.shape[1] // 2 + column
    copies = []
    for kind, (low, target) in enumerate(((value_column, values), (column, keys))):
        for b, source in enumerate((older_ref, old_ref, own_ref)):
            for i in range(PAIR):
                place = pl.multiple_of(numbers[i] + b * PAIR * rows, rows)
                copies.append(
                    pltpu.make_async_copy(
                        source.at[pl.ds(i * rows, rows), pl.ds(low, HEAD_WIDTH)],
                        target.at[pl.ds(place, rows)],
                        sems.at[kind, b * PAIR + i],
                    )
                )
    for copy in copies:
        copy.start()
    turned[HEAD_WIDTH:] = jnp.ones(
        (turned.shape[0] - HEAD_WIDTH, turned.shape[1]), jnp.bfloat16
    )
    longest[...] = jnp.zeros(longest.shape, jnp.float32)
    for copy in copies:
        copy.wait()

    def turn(i, carry):
        part = pl.ds(pl.multiple_of(i * KEY_TILE, KEY_TILE), KEY_TILE)
        turned[:HEAD_WIDTH, part] = values[part].T
        longest[...] = jnp.maximum(longest[...], largest_square(keys[part]))
        return carry

    lax.fori_loop(0, keys.shape[0] // KEY_TILE, turn, 0)


def window(column, numbers, older, old, own):
    key_total = 3 * own.shape[0]
    vmem = pl.BlockSpec(memory_space=pltpu.VMEM)
    return pl.pallas_call(
        functools.partial(window_kernel, column),
        out_shape=(
            jax.ShapeDtypeStruct((key_total, HEAD_WIDTH), jnp.bfloat16),
            jax.ShapeDtypeStruct((HEAD_WIDTH + 16, key_total), jnp.bfloat16),
            jax.ShapeDtypeStruct((1, HEAD_WIDTH), jnp.float32),
        ),
        in_specs=[pl.BlockSpec(memory_space=pltpu.SMEM)]
        + [pl.BlockSpec(memory_space=pl.ANY)] * 3,
        out_specs=(vmem, vmem, vmem),
        scratch_shapes=[
            pltpu.VMEM((key_total, HEAD_WIDTH), jnp.bfloat16),
            pltpu.SemaphoreType.DMA((2, 3 * PAIR)),
        ],
        compiler_params=pltpu.CompilerParams(vmem_limit_bytes=60 * 1024 * 1024),
        cost_estimate=pl.CostEstimate(flops=1000, bytes_accessed=1000, transcendentals=0),
        name="window",
    )(numbers, older, old, own)


def attend_kernel(
    numbers, start_ref, query_ref, keys, turned, longest, out_ref, total, top_ref
):
    step = pl.program_id(0)
    tiles = pl.num_programs(0)
    _, tile_rows, width = query_ref.shape
    group = width // HEAD_WIDTH
    first_token = numbers[step]
    low_start = numbers[tiles + step]
    base = numbers[2 * tiles]
    factor = math.log2(math.e) / math.sqrt(HEAD_WIDTH)
    queries = [query_ref[0, :, h * HEAD_WIDTH : (h + 1) * HEAD_WIDTH] for h in range(group)]
    together = jnp.concatenate(queries, axis=0)
    bound = largest_square(together)
    small = jnp.max(bound * longest[...]) * (factor * factor) < SAFE_POWER * SAFE_POWER
    total[...] = jnp.zeros(total.shape, jnp.float32)
    top_ref[...] = jnp.full(top_ref.shape, LOWEST, jnp.float32)

    def add(tile, careful):
        low = pl.multiple_of(tile * KEY_TILE, KEY_TILE)
        here = keys[pl.ds(low, KEY_TILE)]
        shape = (KEY_TILE, tile_rows)
        key_index = base + low + lax.broadcasted_iota(jnp.int32, shape, 0)
        token = first_token + lax.broadcasted_iota(jnp.int32, shape, 1)
        seen = (key_index <= token) & (key_index >= start_ref[0])
        scores = lax.dot_general(
            here, together, (((1,), (1,)), ((), ())), preferred_element_type=jnp.float32
        )
        scores = scores * factor
        power = jnp.concatenate(
            [
                jnp.where(seen, scores[:, h * tile_rows : (h + 1) * tile_rows], LOWEST)
                for h in range(group)
            ],
            axis=1,
        )
        before = total[...]
        if careful:
            old_top = top_ref[...]
            new_top = jnp.maximum(old_top, jnp.max(power, axis=0, keepdims=True))
            top_ref[...] = new_top
            power = power - new_top
            before = before * jnp.exp2(old_top - new_top)
        total[...] = before + jnp.dot(
            turned[:, pl.ds(low, KEY_TILE)],
            jnp.exp2(power).astype(jnp.bfloat16),
            preferred_element_type=jnp.float32,
        )

    def plain_tile(tile, carry):
        add(tile, False)
        return carry

    def careful_tile(tile, carry):
        add(tile, True)
        return carry

    from_tile = (low_start - base) // KEY_TILE
    to_tile = (first_token + tile_rows - 1 - base) // KEY_TILE + 1
    middle = jnp.where(small, to_tile, from_tile)
    lax.fori_loop(from_tile, middle, plain_tile, 0)
    lax.fori_loop(middle, to_tile, careful_tile, 0)
    for h in range(group):
        columns = pl.ds(h * tile_rows, tile_rows)
        mixed = total[:HEAD_WIDTH, columns] / total[HEAD_WIDTH : HEAD_WIDTH + 1, columns]
        out_ref[0, :, h * HEAD_WIDTH : (h + 1) * HEAD_WIDTH] = mixed.astype(jnp.bfloat16).T


def attend(numbers, tile_starts, queries, keys, turned, longest):
    tiles, tile_rows, width = queries.shape
    group = width // HEAD_WIDTH
    deep = turned.shape[0]

    def whole(array):
        return pl.BlockSpec(array.shape, lambda i, n: (0, 0))

    return pl.pallas_call(
        attend_kernel,
        grid_spec=pltpu.PrefetchScalarGridSpec(
            num_scalar_prefetch=1,
            grid=(tiles,),
            in_specs=[
                pl.BlockSpec((1, 1, tile_rows), lambda i, n: (i, 0, 0)),
                pl.BlockSpec((1, tile_rows, width), lambda i, n: (i, 0, 0)),
                whole(keys),
                whole(turned),
                whole(longest),
            ],
            out_specs=pl.BlockSpec((1, tile_rows, width), lambda i, n: (i, 0, 0)),
            scratch_shapes=[
                pltpu.VMEM((deep, group * tile_rows), jnp.float32),
                pltpu.VMEM((1, group * tile_rows), jnp.float32),
            ],
        ),
        out_shape=jax.ShapeDtypeStruct(queries.shape, jnp.bfloat16),
        compiler_params=pltpu.CompilerParams(vmem_limit_bytes=60 * 1024 * 1024),
        cost_estimate=pl.CostEstimate(flops=1000, bytes_accessed=1000, transcendentals=0),
        name="attend",
    )(numbers, tile_starts, queries, keys, turned, longest)


def place_kernel(numbers, *refs):
    sources, outs, (held, sems, out_sems) = refs[:-5], refs[-5:-3], refs[-3:]
    width = sources[0].shape[2]
    each = len(sources) // len(outs)
    copies = [
        pltpu.make_async_copy(
            source.at[numbers[2 * n]],
            held.at[n // each, :, pl.ds(pl.multiple_of(numbers[2 * n + 1], width), width)],
            sems.at[n],
        )
        for n, source in enumerate(sources)
    ]
    for copy in copies:
        copy.start()
    last = [
        pltpu.make_async_copy(held.at[kind], out, out_sems.at[kind])
        for kind, out in enumerate(outs)
    ]
    for kind, whole in enumerate(last):
        for copy in copies[kind * each : (kind + 1) * each]:
            copy.wait()
        whole.start()
    for whole in last:
        whole.wait()


def place(blocks, columns):
    numbers = jnp.stack([n for _, index, low in blocks for n in (index, low)]).astype(jnp.int32)
    arrays = [array for array, _, _ in blocks]
    _, rows, _ = arrays[0].shape
    return pl.pallas_call(
        place_kernel,
        out_shape=(jax.ShapeDtypeStruct((rows, columns), arrays[0].dtype),) * 2,
        in_specs=[pl.BlockSpec(memory_space=pltpu.SMEM)]
        + [pl.BlockSpec(memory_space=pl.ANY)] * len(blocks),
        out_specs=(pl.BlockSpec(memory_space=pl.ANY),) * 2,
        scratch_shapes=[
            pltpu.VMEM((2, rows, columns), arrays[0].dtype),
            pltpu.SemaphoreType.DMA((len(blocks),)),
            pltpu.SemaphoreType.DMA((2,)),
        ],
        compiler_params=pltpu.CompilerParams(vmem_limit_bytes=60 * 1024 * 1024),
        cost_estimate=pl.CostEstimate(flops=1000, bytes_accessed=1000, transcendentals=0),
        name="place",
    )(numbers, *arrays)


def pair_body(
    hidden,
    attention_norm_gain,
    wq,
    adapter_down_weight,
    adapter_up_weight,
    key_value_cache,
    logical_page_table,
    lengths,
    prompt_adapter_index,
):
    rows, features = hidden.shape
    count = lax.axis_size("page")
    me = lax.axis_index("page")
    core, x, y, z = me % 2, (me // 2) % 2, (me // 4) % 2, me // 8
    pair = me // PAIR
    quarter = me % PAIR
    q_cols = wq.shape[1]
    width = q_cols // PAIR
    kv_width = key_value_cache.shape[2]
    kv_part = kv_width // PAIR
    kv_heads = kv_part // HEAD_WIDTH
    chunk = width // kv_heads

    def weight_part(part_x, part_core):
        return lax.dynamic_slice_in_dim(wq, (2 * part_x + part_core) * width, width, 1)

    sent = Transfers()
    core_swap = functools.partial(swap, bit=1)
    x_swap = functools.partial(swap, bit=2)
    y_swap = functools.partial(swap, bit=4)
    wq_rows = wq.shape[0]
    wq_depth = PAIR * wq_rows
    pairs = count // PAIR
    z_count = count // 8
    order = (0, 1, 3, 2)

    rank = adapter_up_weight.shape[0]
    slots = prompt_adapter_index.shape[0]
    part = width // pairs
    both = jnp.concatenate([adapter_down_weight.T, adapter_up_weight], axis=0)
    both = both.reshape(2 * rank, PAIR, pairs, part).transpose(2, 1, 0, 3)
    both = both.reshape(count * 2 * rank, part)

    def exchange(value):
        return lax.all_to_all(value, "page", split_axis=0, concat_axis=0, tiled=True)

    sent.run([], [("adapters", both, exchange)])
    sent.run(
        [],
        [
            (
                "weight c",
                jnp.concatenate([weight_part(x, 1 - core), weight_part(1 - x, 1 - core)], axis=0),
                core_swap,
            )
        ],
    )
    from_core = sent["weight c"]
    mine = in_order(core, weight_part(1 - x, core), from_core[wq_rows:])
    kept = in_order(core, weight_part(x, core), from_core[:wq_rows])
    first_mine, key_value_cache = lax.optimization_barrier((mine[:, :chunk], key_value_cache))
    sent.run([], [("weight x0", first_mine, x_swap)])
    (hidden,) = sent.tie([hidden], ["weight x0"])

    page_count = logical_page_table.shape[1]
    page_rows = rows // page_count
    paged = key_value_cache.reshape(page_count, page_rows, 2, kv_width)
    ordered = jnp.concatenate(
        [
            lax.dynamic_index_in_dim(paged, logical_page_table[0, j], 0, keepdims=False)
            for j in range(page_count)
        ],
        axis=0,
    ).reshape(rows, 2 * kv_width)

    def cache_part(part_x, part_core):
        low = (2 * part_x + part_core) * kv_part
        return jnp.concatenate(
            [
                lax.dynamic_slice_in_dim(ordered, low, kv_part, 1),
                lax.dynamic_slice_in_dim(ordered, kv_width + low, kv_part, 1),
            ],
            axis=1,
        )

    sent.run(
        [],
        [
            (
                "cache c",
                jnp.concatenate([cache_part(x, 1 - core), cache_part(1 - x, 1 - core)], axis=0),
                core_swap,
            )
        ],
    )
    cache_core = sent["cache c"]

    wide = hidden.astype(jnp.float32)
    scale_rows = lax.rsqrt(jnp.mean(wide * wide, axis=-1, keepdims=True) + EPSILON)
    normed_own = (wide * scale_rows * attention_norm_gain.astype(jnp.float32)).astype(jnp.bfloat16)
    half_rows = rows // 2
    ends = jnp.cumsum(lengths)
    starts = ends - lengths
    first_token = pair * (PAIR * rows)
    token = first_token + jnp.arange(PAIR * rows, dtype=jnp.int32)
    member = (token[None, :] >= starts[:, None]) & (token[None, :] < ends[:, None])
    tok_start = jnp.sum(jnp.where(member, starts[:, None], 0), axis=0)
    position = (token - tok_start).astype(jnp.float32)
    half = HEAD_WIDTH // 2
    inverse = ROPE_BASE ** (-(jnp.arange(half, dtype=jnp.float32) * 2.0 / HEAD_WIDTH))
    angle = position[:, None] * inverse[None, :]
    cosine, sine = jnp.cos(angle), jnp.sin(angle)
    cosine = jnp.concatenate([cosine, cosine], axis=1).reshape(PAIR, rows, HEAD_WIDTH)
    sine = jnp.concatenate([-sine, sine], axis=1).reshape(PAIR, rows, HEAD_WIDTH)

    chosen = choose(prompt_adapter_index, sent["adapters"].reshape(count, 2 * rank, part), chunk)
    pieces = [in_order(x, kept[:, :chunk], sent["weight x0"])]

    def along_z(g, k):
        return (f"z{g} {k}", pieces[g], functools.partial(shift_z, steps=k))

    def along_y(g, k):
        return (f"y{g} {k}", sent[f"z{g} {k}"] if k else pieces[g], y_swap)

    def older(value):
        return lax.ppermute(value, "page", [(p, p + 8) for p in range(count - 8)])

    cuts = (0, rows // 2, rows)

    def normed_part(n):
        return (f"normed x{n}", normed_own[cuts[n] : cuts[n + 1]], x_swap)

    def normed_on(n):
        return (f"normed xc{n}", sent[f"normed x{n}"], core_swap)

    sent.run(
        ["weight x0"],
        [
            along_z(0, 1),
            along_z(0, 3),
            along_y(0, 0),
            ("weight x1", mine[:, chunk:], x_swap),
        ],
    )
    sent.run(
        [],
        [
            ("normed c", normed_own, core_swap),
            (
                "cache x",
                jnp.concatenate([cache_part(1 - x, core), cache_core[rows:]], axis=0),
                x_swap,
            ),
        ],
    )
    pieces.append(in_order(x, kept[:, chunk:], sent["weight x1"]))
    sent.run(
        ["z0 1", "z0 3", "y0 0", "weight x1", "cache x", "normed c"],
        [
            along_z(0, 2),
            along_z(1, 1),
            ("y0 1 3", jnp.concatenate([sent["z0 1"], sent["z0 3"]], axis=0), y_swap),
            along_y(1, 0),
            normed_part(0),
        ]
        + [
            (f"adapters z{k}", chosen, functools.partial(shift_z, steps=k)) for k in order[1:]
        ],
    )
    cache_own = jnp.concatenate([cache_part(x, core), cache_core[:rows], sent["cache x"]], axis=0)
    cosine, sine = sent.tie([cosine, sine], ["y1 0"])
    sent.run(
        ["z0 2", "z1 1", "y0 1 3", "y1 0", "normed x0"]
        + [f"adapters z{k}" for k in order[1:]],
        [
            ("cache z", cache_own, older),
            along_y(0, 2),
            along_y(1, 1),
            normed_part(1),
            normed_on(0),
            (
                "adapters y",
                jnp.concatenate(
                    [chosen] + [sent[f"adapters z{k}"] for k in order[1:]], axis=0
                ),
                y_swap,
            ),
        ],
    )
    adapters_near = jnp.concatenate(
        [chosen] + [sent[f"adapters z{k}"] for k in order[1:]], axis=0
    )
    sent.run(
        ["cache z", "y0 2", "y1 1", "normed x1", "normed xc0", "adapters y"],
        [
            normed_on(1),
            along_z(1, 3),
            along_z(1, 2),
            ("cache y", jnp.where(y == 1, sent["cache z"], cache_own), y_swap),
        ],
    )
    normed = [normed_own, sent["normed c"]]
    normed += [sent[f"normed {way}{n}"] for way in ("x", "xc") for n in range(2)]
    layout = ((0, 0), (1, 0)) + tuple((i, cuts[n]) for i in (2, 3) for n in range(2))

    members = jnp.arange(PAIR, dtype=jnp.int32)
    places = [((z - k) % z_count) * 2 + (y ^ dy) for k in order for dy in (0, 1)]
    numbers = jnp.concatenate(
        [
            quarter[None],
            jnp.stack(places),
            first_token + (quarter ^ members) * rows,
            starts,
            ends,
        ]
    ).astype(jnp.int32)
    partial, up = shrink(
        numbers,
        layout,
        normed,
        adapters_near,
        sent["adapters y"],
        2 * z_count,
        part,
        slots,
        rank,
    )
    partial = partial + swap(partial, 1)
    partial = partial + swap(partial, 2)
    shrunk = partial.astype(jnp.bfloat16)

    def project_part(g, spots, weights, shrunk):
        return project(
            numbers, layout, spots, normed, weights, shrunk, up[:, g * chunk : (g + 1) * chunk], cosine, sine
        )

    block_starts = jnp.stack(
        [lax.dynamic_slice_in_dim(tok_start, (quarter ^ i) * rows, rows, 0) for i in range(PAIR)]
    ).reshape(PAIR, 1, rows)

    def attend_part(g, first, queries):
        tiles = queries.shape[0]
        here = block_starts[first : first + tiles]
        steps = jnp.concatenate(
            [
                first_token + (quarter ^ members[first : first + tiles]) * rows,
                here[:, 0, 0],
                (first_token - 2 * PAIR * rows)[None],
            ]
        ).astype(jnp.int32)
        return attend(steps, here, queries, *windows[g])

    def home(name, g, value):
        from_x = sent[f"{name} x{g}"]
        from_core = swap(jnp.stack([value[1], from_x[1]]), 1)
        found = ((0, value, 0), (2, from_x, 0), (1, from_core, 0), (3, from_core, 1))
        return [
            (array, jnp.int32(which), (quarter ^ bits) * width + g * chunk)
            for bits, array, which in found
        ]

    depth = wq_depth
    home0, away0 = project_part(
        0,
        ((0, 0), (1, 0), (2, 0), (5, 0), (3, 0), (5, depth), (4, 0), (6, 0)),
        [pieces[0]]
        + [sent[name] for name in ("y0 0", "z0 1", "z0 3", "z0 2", "y0 1 3", "y0 2")],
        shrunk,
    )
    away0, home0, cache_old = lax.optimization_barrier((away0, home0, sent["cache y"]))
    windows = [
        window(
            g * HEAD_WIDTH,
            ((quarter ^ members) * rows).astype(jnp.int32),
            sent["cache z"],
            cache_old,
            cache_own,
        )
        for g in range(kv_heads)
    ]

    sent.run([], [("queries x0", away0, x_swap)])
    attended_away0 = attend_part(0, 2, away0)
    attended_away0, last3, last2 = lax.optimization_barrier(
        (attended_away0, sent["z1 3"], sent["z1 2"])
    )
    sent.run(
        ["cache y"],
        [
            ("y1 3 2", jnp.concatenate([last3, last2], axis=0), y_swap),
            ("attended x0", attended_away0, x_swap),
        ],
    )
    attended_home0 = attend_part(0, 0, home0)
    shrunk, attended_home0, *windows[1] = lax.optimization_barrier(
        (shrunk, attended_home0, *windows[1])
    )
    (shrunk,) = sent.tie([shrunk], ["queries x0"])
    home1, away1 = project_part(
        1,
        ((0, 0), (1, 0), (2, 0), (5, 0), (3, 0), (6, 0), (4, 0), (6, depth)),
        [pieces[1]]
        + [sent[name] for name in ("y1 0", "z1 1", "z1 3", "z1 2", "y1 1", "y1 3 2")],
        shrunk,
    )
    sent.run([], [("queries x1", away1, x_swap)])
    (away1,) = sent.tie([away1], ["attended x0"])
    attended_away1 = attend_part(1, 2, away1)
    sent.run(["queries x1"], [("attended x1", attended_away1, x_swap)])
    attended_home1 = attend_part(1, 0, home1)
    return tuple(
        place(
            home("queries", 0, home0)
            + home("queries", 1, home1)
            + home("attended", 0, attended_home0)
            + home("attended", 1, attended_home1),
            q_cols,
        )
    )


def solution(mesh):
    page, head = mesh.shape["page"], mesh.shape["head"]
    return jax.shard_map(
        pair_body if head == 1 and page == 32 else body,
        mesh=mesh,
        in_specs=(
            P("page", None),
            P(),
            P("page", "head"),
            P("head", "page"),
            P("page", "head"),
            P("page", None, "head"),
            P("page", None),
            P(),
            P(),
        ),
        out_specs=(P("page", "head"), P("page", "head")),
        check_vma=False,
    )
```
